512 devices in a mesh: head: 2 (over y_hi), view: 16 (over z), row: 16 (over y_lo, x, core).
Axes of the slice: x: 4, y: 4 (y_hi: 2, y_lo: 2; y = y_hi * 2 + y_lo), z: 16, core: 2. Of those that a mesh axis runs over, the one named last changes fastest.
Arguments:
- query_feats: bfloat16 [16, 128, 16, 1024], P('view', 'row', None, 'head'), may hold values from -125 to 125
- key_feats: bfloat16 [16, 128, 16, 1024], P('view', 'row', None, 'head'), may hold values from -7 to 7
- value_feats: bfloat16 [16, 128, 16, 1024], P('view', 'row', None, 'head'), may hold values from -6 to 6
- target: bfloat16 [16, 128, 16, 1024], P('view', 'row', None, 'head'), may hold values from -6 to 6
- token_rates: float32 [16, 2, 2048], P('view', 'head', 'row'), may hold values from 5 to 100
- row_reach: int32 [128], P('row'), may hold values from 1 to 2
- view_counts: int32 [16], P('view'), may hold values from 682 to 2048
- w_first: bfloat16 [2, 512, 512], P('head'), may hold values from -0.25 to 0.25
- w_third: bfloat16 [2, 512, 512], P('head'), may hold values from -0.25 to 0.25
- w_second: bfloat16 [2, 512, 512], P('head'), may hold values from -0.25 to 0.25
Outputs:
- fast_out: bfloat16 [16, 128, 16, 1024], P('view', 'row', None, 'head')
The draws below stay inside these ranges and needn't reach their ends.
All inputs are finite; a program needn't handle non-finite values.
Results may differ from the reference program's by a relative error of at most 0.03.
Values may be sent and summed in bfloat16 or wider, within the bound.
No kernel may reach another device: no remote copies, remote signals or barrier semaphores. Data moves between devices by JAX's collectives and lax.ppermute only.
A program may use at most 64 MiB of HBM per device.

```python
import math
import jax
import jax.numpy as jnp
from jax import lax

HEADS = 2
HD = 512
ATT_HD = 128
COLS = 16
ROWS_DEV = 8
HALO = 2
NR = 128
VIEWS = 16
VIEW_TOK = 2048


def draw_pair(key):
    grid_shape = (VIEWS, NR, COLS, HEADS * HD)
    keys_draw = jax.random.truncated_normal(jax.random.fold_in(key, 11), -6.0, 6.0, grid_shape, jnp.float32)
    query_draw = jax.random.truncated_normal(jax.random.fold_in(key, 12), -6.0, 6.0, grid_shape, jnp.float32)
    return (query_draw, keys_draw)


def draw_query_feats(key, part):
    return draw_pair(key)[0].astype(jnp.bfloat16)


def draw_key_feats(key, part):
    return draw_pair(key)[1].astype(jnp.bfloat16)


def draw_view_counts(key, part):
    position = jnp.arange(VIEWS, dtype=jnp.int32)
    lowest = VIEW_TOK // 3
    growth = (VIEW_TOK - lowest - VIEW_TOK // 8) * position // max(VIEWS - 1, 1)
    jitter = jax.random.randint(key, (VIEWS,), 0, VIEW_TOK // 8 + 1, jnp.int32)
    return jnp.minimum(lowest + growth + jitter, VIEW_TOK).astype(jnp.int32)


def plant(values, stream_key, low, high):
    spot = [jax.random.randint(jax.random.fold_in(stream_key, axis), (), 0, length) for axis, length in enumerate(values.shape)]
    widest = values.shape.index(max(values.shape))
    beside = spot[:widest] + [(spot[widest] + 1) % values.shape[widest]] + spot[widest + 1:]
    return values.at[tuple(spot)].set(low).at[tuple(beside)].set(high)


def block_levels(rng, dims, split, low, top_value):
    loudness, own = 1.0, jax.random.fold_in(rng, 6)
    for dim, shards_of in split:
        draws = jnp.exp(jax.random.uniform(jax.random.fold_in(own, dim), (shards_of,), jnp.float32, low / len(split), top_value / len(split)))
        loudness = loudness * jnp.repeat(draws, dims[dim] // shards_of).reshape([-1 if axis == dim else 1 for axis in range(len(dims))])
    return loudness


def noise(rng, dims, scale, reach, split=(), held_as=jnp.bfloat16):
    entries = scale * jax.random.normal(rng, dims, jnp.float32)
    if split:
        entries = entries * block_levels(rng, dims, split, -0.22, 0.18)
    return jnp.clip(entries, -reach, reach).astype(held_as)


def setup_inputs(seed: int = 0) -> dict:
    splits = jax.random.split(jax.random.key(seed), 11)
    return {
        "query_feats": draw_query_feats(jax.random.fold_in(splits[10], 71), 0),
        "key_feats": draw_key_feats(jax.random.fold_in(splits[10], 71), 0),
        "value_feats": noise(splits[2], (VIEWS, NR, COLS, HEADS * HD), 1.0, 6.0, ((0, 16), (1, 16), (3, 2))),
        "target": noise(splits[3], (VIEWS, NR, COLS, HEADS * HD), 1.0, 6.0, ((0, 16), (1, 16), (3, 2))),
        "token_rates": jnp.clip(jnp.exp(math.log(100.0) - 2.9957323 * jax.random.uniform(splits[4], (VIEWS, HEADS, NR * COLS), jnp.float32) ** block_levels(splits[4], (VIEWS, HEADS, NR * COLS), ((0, 16), (1, 2), (2, 16)), -0.2, 0.2)), 5.0, 100.0),
        "row_reach": plant(jax.random.randint(splits[5], (NR,), 1, 3), jax.random.fold_in(splits[5], 1), 1, 2).astype(jnp.int32),
        "view_counts": draw_view_counts(jax.random.fold_in(splits[10], 71), 0),
        "w_first": noise(splits[7], (HEADS, HD, HD), HD ** -0.5, 0.25, ((0, 2),)),
        "w_third": noise(splits[8], (HEADS, HD, HD), HD ** -0.5, 0.25, ((0, 2),)),
        "w_second": noise(splits[9], (HEADS, HD, HD), HD ** -0.5, 0.25, ((0, 2),)),
    }


def silu_slope(values_in):
    sigmoid_x = jax.nn.sigmoid(values_in)
    return sigmoid_x * (1.0 + values_in * (1.0 - sigmoid_x))

def attend(query_rows, key_rows, value_rows, q_row_ids, k_row_ids, q_tok, k_tok, k_valid, q_reach, grid_rows):
    count_q = query_rows.shape[0]
    count_k = key_rows.shape[0]
    groups = query_rows.shape[1] // ATT_HD
    query_heads = query_rows.reshape(count_q, groups, ATT_HD).astype(jnp.float32)
    key_heads = key_rows.reshape(count_k, groups, ATT_HD).astype(jnp.float32)
    value_heads = value_rows.reshape(count_k, groups, ATT_HD).astype(jnp.float32)
    scores = jnp.einsum('qhd,khd->hqk', query_heads, key_heads) / math.sqrt(ATT_HD)
    inside = (k_row_ids >= 0) & (k_row_ids < grid_rows)
    in_band = jnp.abs(k_row_ids[None, :] - q_row_ids[:, None]) <= q_reach[:, None]
    allowed = in_band & inside[None, :] & (k_valid[None, :] | (k_tok[None, :] == q_tok[:, None]))
    scores = jnp.where(allowed[None], scores, -1e+30)
    row_top = lax.optimization_barrier(jnp.max(scores, -1, keepdims=True))
    powers = jnp.exp(scores - row_top)
    weights = (powers / lax.optimization_barrier(jnp.sum(powers, -1, keepdims=True))).astype(jnp.bfloat16)
    output_rows = jnp.einsum('hqk,khd->qhd', weights.astype(jnp.float32), value_heads)
    return output_rows.reshape(count_q, groups * ATT_HD).astype(jnp.bfloat16)

def renorm(old_matrix, grad, total_valid):
    old_rows = old_matrix.astype(jnp.float32)
    raised = old_rows + grad / total_valid
    rescale = jnp.sqrt(lax.optimization_barrier(jnp.sum(old_rows * old_rows, -1, keepdims=True)) + 1e-06) / jnp.sqrt(lax.optimization_barrier(jnp.sum(raised * raised, -1, keepdims=True)) + 1e-06)
    return (raised * rescale).astype(jnp.bfloat16)

def reference(query_feats, key_feats, value_feats, target, token_rates, row_reach, view_counts, w_first, w_third, w_second):
    feat_width = HEADS * HD
    row_pad = ((0, 0), (HALO, HALO), (0, 0), (0, 0))
    key_pad = jnp.pad(key_feats, row_pad)
    value_pad = jnp.pad(value_feats, row_pad)
    blocks = NR // ROWS_DEV
    key_span = ROWS_DEV + 2 * HALO

    def attend_block(flat_index):
        view_index = (flat_index // blocks).astype(jnp.int32)
        row_start = (flat_index % blocks * ROWS_DEV).astype(jnp.int32)
        zero_index = jnp.zeros((), jnp.int32)
        q_blk = lax.dynamic_slice(query_feats, (view_index, row_start, zero_index, zero_index), (1, ROWS_DEV, COLS, feat_width))[0].reshape(ROWS_DEV * COLS, feat_width)
        k_blk = lax.dynamic_slice(key_pad, (view_index, row_start, zero_index, zero_index), (1, key_span, COLS, feat_width))[0].reshape(key_span * COLS, feat_width)
        v_blk = lax.dynamic_slice(value_pad, (view_index, row_start, zero_index, zero_index), (1, key_span, COLS, feat_width))[0].reshape(key_span * COLS, feat_width)
        q_row_ids = row_start + jnp.repeat(jnp.arange(ROWS_DEV, dtype=jnp.int32), COLS)
        k_row_ids = row_start - HALO + jnp.repeat(jnp.arange(key_span, dtype=jnp.int32), COLS)
        q_tok = q_row_ids * COLS + jnp.tile(jnp.arange(COLS, dtype=jnp.int32), ROWS_DEV)
        k_tok = k_row_ids * COLS + jnp.tile(jnp.arange(COLS, dtype=jnp.int32), key_span)
        view_total = view_counts[view_index]
        k_valid = k_tok < view_total
        q_reach = row_reach[q_row_ids]
        return attend(q_blk, k_blk, v_blk, q_row_ids, k_row_ids, q_tok, k_tok, k_valid, q_reach, NR)
    blocks_out = lax.map(attend_block, jnp.arange(VIEWS * blocks, dtype=jnp.int32))
    total_tok = VIEWS * NR * COLS
    attended = blocks_out.reshape(total_tok, HEADS, HD).astype(jnp.float32)
    fast_keys = (attended * lax.rsqrt(lax.optimization_barrier(jnp.mean(attended * attended, -1, keepdims=True)) + 1e-06)).astype(jnp.bfloat16)
    tok_index = jnp.arange(NR * COLS, dtype=jnp.int32)
    valid_mask = (tok_index[None, :] < view_counts[:, None]).reshape(total_tok).astype(jnp.float32)
    rates_tok = jnp.transpose(token_rates, (0, 2, 1)).reshape(total_tok, HEADS)
    scaled = (rates_tok[:, :, None] * valid_mask[:, None, None] * target.reshape(total_tok, HEADS, HD).astype(jnp.float32)).astype(jnp.bfloat16)
    total_valid = jnp.sum(view_counts).astype(jnp.float32)
    results = []
    for head in range(HEADS):
        key_rows = fast_keys[:, head]
        scaled_rows = scaled[:, head]
        first_proj = jnp.dot(key_rows, w_first[head], preferred_element_type=jnp.float32)
        third_proj = jnp.dot(key_rows, w_third[head], preferred_element_type=jnp.float32)
        gated_rows = (jax.nn.silu(first_proj) * third_proj).astype(jnp.bfloat16)
        back_rows = lax.dot_general(scaled_rows, w_second[head], (((1,), (1,)), ((), ())), preferred_element_type=jnp.float32)
        back_first = (back_rows * third_proj * silu_slope(first_proj)).astype(jnp.bfloat16)
        back_third = (back_rows * jax.nn.silu(first_proj)).astype(jnp.bfloat16)
        grad_first = jnp.dot(key_rows.T, back_first, preferred_element_type=jnp.float32)
        grad_third = jnp.dot(key_rows.T, back_third, preferred_element_type=jnp.float32)
        grad_second = jnp.dot(gated_rows.T, scaled_rows, preferred_element_type=jnp.float32)
        new_first = renorm(w_first[head], grad_first, total_valid)
        new_third = renorm(w_third[head], grad_third, total_valid)
        new_second = renorm(w_second[head], grad_second, total_valid)
        applied = (jax.nn.silu(jnp.dot(key_rows, new_first, preferred_element_type=jnp.float32)) * jnp.dot(key_rows, new_third, preferred_element_type=jnp.float32)).astype(jnp.bfloat16)
        results.append(jnp.dot(applied, new_second, preferred_element_type=jnp.float32).astype(jnp.bfloat16))
    return jnp.stack(results, 1).reshape(VIEWS, NR, COLS, HEADS * HD)
```

```python
import math

import jax
import jax.numpy as jnp
from jax import lax
from jax.sharding import Mesh
from jax.sharding import PartitionSpec as P

HD = 512
ATT_HD = 128
HALO = 2
PLANE = ("row_0", "row_1")
ROW = ("row_0", "row_1", "row_2")
SWAP = [(0, 1), (1, 0)]
BF = jnp.bfloat16
F32 = jnp.float32


def silu_slope(values_in):
    sigmoid_x = jax.nn.sigmoid(values_in)
    return sigmoid_x * (1.0 + values_in * (1.0 - sigmoid_x))


def attend(query_rows, key_rows, value_rows, q_row_ids, k_row_ids, q_tok, k_tok, k_valid, q_reach, grid_rows):
    count_q = query_rows.shape[0]
    count_k = key_rows.shape[0]
    groups = query_rows.shape[1] // ATT_HD
    query_heads = query_rows.reshape(count_q, groups, ATT_HD)
    key_heads = key_rows.reshape(count_k, groups, ATT_HD)
    value_heads = value_rows.reshape(count_k, groups, ATT_HD)
    scores = jnp.einsum("qhd,khd->hqk", query_heads, key_heads, preferred_element_type=F32) / math.sqrt(ATT_HD)
    inside = (k_row_ids >= 0) & (k_row_ids < grid_rows)
    in_band = jnp.abs(k_row_ids[None, :] - q_row_ids[:, None]) <= q_reach[:, None]
    allowed = in_band & inside[None, :] & (k_valid[None, :] | (k_tok[None, :] == q_tok[:, None]))
    scores = jnp.where(allowed[None], scores, -1e30)
    row_top = jnp.max(scores, -1, keepdims=True)
    powers = jnp.exp(scores - row_top)
    weights = (powers / jnp.sum(powers, -1, keepdims=True)).astype(BF)
    output_rows = jnp.einsum("hqk,khd->qhd", weights, value_heads, preferred_element_type=F32)
    return output_rows.reshape(count_q, groups * ATT_HD).astype(BF)


def dot(a, b, ca=1, cb=0):
    return lax.dot_general(a, b, (((ca,), (cb,)), ((), ())), preferred_element_type=F32)


def exchange(x, axes):
    return lax.all_to_all(x, axes, 0, 0, tiled=True)


def to_all(x, axes):
    return exchange(jnp.broadcast_to(x[None], (lax.axis_size(axes), *x.shape)), axes)


def halves(x, core):
    w = x.shape[1] // 2
    left, right = x[:, :w], x[:, w:]
    return jnp.where(core == 0, left, right), jnp.where(core == 0, right, left)


def per_device(query_feats, key_feats, value_feats, target, token_rates, row_reach, view_counts, w_first, w_third, w_second):
    _, rows, cols, width = query_feats.shape
    tokens = rows * cols
    span = rows + 2 * HALO
    n_row = lax.axis_size(ROW)
    grid_rows = n_row * rows
    core = lax.axis_index("row_2")
    plane = lax.axis_index(PLANE)
    view = lax.axis_index("view")
    n_plane, n_view = lax.axis_size(PLANE), lax.axis_size("view")
    row_base = lax.axis_index(ROW) * rows
    count = view_counts[0]

    paired = jnp.stack([key_feats[0], value_feats[0]], 0)
    leading, last = paired[:, :HALO], paired[:, rows - HALO :]
    to_core = jnp.where(core == 0, last, leading)
    to_chip = jnp.where(core == 0, leading, last)
    next_chip = [p for i in range(1, n_row - 1, 2) for p in ((i, i + 1), (i + 1, i))]
    from_core = lax.ppermute(to_core, "row_2", SWAP)
    from_chip = lax.ppermute(to_chip, ROW, next_chip)
    before = jnp.where(core == 0, from_chip, from_core)
    after = jnp.where(core == 0, from_core, from_chip)
    padded = jnp.concatenate([before, paired, after], 1)

    q_row_ids = row_base + jnp.repeat(jnp.arange(rows, dtype=jnp.int32), cols)
    k_row_ids = row_base - HALO + jnp.repeat(jnp.arange(span, dtype=jnp.int32), cols)
    q_tok = row_base * cols + jnp.arange(tokens, dtype=jnp.int32)
    k_tok = (row_base - HALO) * cols + jnp.arange(span * cols, dtype=jnp.int32)
    attended = attend(
        query_feats[0].reshape(tokens, width),
        padded[0].reshape(span * cols, width),
        padded[1].reshape(span * cols, width),
        q_row_ids,
        k_row_ids,
        q_tok,
        k_tok,
        k_tok < count,
        jnp.repeat(row_reach, cols),
        grid_rows,
    ).astype(F32)
    fast_keys = (attended * lax.rsqrt(jnp.mean(attended * attended, -1, keepdims=True) + 1e-06)).astype(BF)
    valid = (q_tok < count).astype(F32)
    scaled = (token_rates[0, 0][:, None] * valid[:, None] * target[0].reshape(tokens, width).astype(F32)).astype(BF)

    own = jnp.stack([fast_keys, scaled], 0)
    both = jnp.concatenate([own, lax.ppermute(own, "row_2", SWAP)], 1)
    keys2, scaled2 = both[0], both[1]
    first = dot(keys2, w_first[0])
    third = dot(keys2, w_third[0])
    back = dot(scaled2, w_second[0], 1, 1)
    gated = (jax.nn.silu(first) * third).astype(BF)
    back_first = (back * third * silu_slope(first)).astype(BF)
    back_third = (back * jax.nn.silu(first)).astype(BF)
    keys_half = halves(keys2, core)[0]
    gated_half = halves(gated, core)[0]
    share = HD // 2 // n_plane
    grads = jnp.concatenate(
        [
            dot(a, b, 0, 0).astype(BF).reshape(n_plane, share, width)
            for a, b in ((keys_half, back_first), (keys_half, back_third), (gated_half, scaled2))
        ],
        1,
    )
    part = exchange(grads, PLANE).astype(F32).sum(0)
    few = share // n_view
    part = part.reshape(3, n_view, few, width).swapaxes(0, 1).reshape(n_view, 3 * few, width)
    digits = jnp.stack([count % 16, (count // 16) % 16, count // 256]).astype(F32)
    lane = jnp.arange(width)
    digit_row = jnp.where(lane == 0, digits[0], jnp.where(lane == 1, digits[1], digits[2]))
    extra = jnp.broadcast_to(digit_row, (n_view, 2, width))
    part = jnp.concatenate([part, extra], 1).astype(BF)
    summed = exchange(part, "view").astype(F32).sum(0)
    total = summed[3 * few, 0] + 16.0 * summed[3 * few, 1] + 256.0 * summed[3 * few, 2]
    grad = summed[: 3 * few].reshape(3, few, width)
    at = core * (HD // 2) + plane * share + view * few
    old = jnp.stack([lax.dynamic_slice_in_dim(w[0], at, few, 0) for w in (w_first, w_third, w_second)]).astype(F32)
    raised = old + grad / total
    rescale = jnp.sqrt(jnp.sum(old * old, -1, keepdims=True) + 1e-06) / jnp.sqrt(
        jnp.sum(raised * raised, -1, keepdims=True) + 1e-06
    )
    new = (raised * rescale).astype(BF).reshape(3 * few, width)
    new = jnp.concatenate([new, jnp.zeros((2, width), BF)], 0)
    lines = to_all(new, "view")[:, : 3 * few].reshape(n_view, 3, few, width).swapaxes(0, 1).reshape(3 * share, width)
    mine = to_all(lines, PLANE)
    theirs = lax.ppermute(mine, "row_2", SWAP)
    m1, m3, m2 = (mine[:, k * share : (k + 1) * share].reshape(HD // 2, width) for k in range(3))
    t1, t3, t2 = (theirs[:, k * share : (k + 1) * share].reshape(HD // 2, width) for k in range(3))
    k_mine, k_theirs = halves(fast_keys, core)
    first = dot(k_mine, m1) + dot(k_theirs, t1)
    third = dot(k_mine, m3) + dot(k_theirs, t3)
    applied = (jax.nn.silu(first) * third).astype(BF)
    a_mine, a_theirs = halves(applied, core)
    out = (dot(a_mine, m2) + dot(a_theirs, t2)).astype(BF)
    return out.reshape(1, rows, cols, width)


def solution(mesh):
    torus = Mesh(
        mesh.devices.reshape(mesh.shape["head"], mesh.shape["view"], 2, 4, 2),
        ("head", "view", "row_0", "row_1", "row_2"),
    )
    feats = P("view", ROW, None, "head")
    heads = P("head", None, None)
    return jax.shard_map(
        per_device,
        mesh=torus,
        in_specs=(feats, feats, feats, feats, P("view", "head", ROW), P(ROW), P("view"), heads, heads, heads),
        out_specs=feats,
        check_vma=False,
    )
```

```python
import math

import jax
import jax.numpy as jnp
from jax import lax
from jax.experimental import pallas as pl
from jax.experimental.pallas import tpu as pltpu
from jax.sharding import Mesh
from jax.sharding import PartitionSpec as P

HD = 512
ATT_HD = 128
HALO = 2
PLANE = ("row_0", "row_1")
ROW = ("row_0", "row_1", "row_2")
SWAP = [(0, 1), (1, 0)]
BF = jnp.bfloat16
F32 = jnp.float32
VMEM = pl.BlockSpec(memory_space=pltpu.VMEM)
SMEM = pl.BlockSpec(memory_space=pltpu.SMEM)


def dot(a, b, ca=1, cb=0):
    return lax.dot_general(a, b, (((ca,), (cb,)), ((), ())), preferred_element_type=F32)


def exchange(x, axes):
    return lax.all_to_all(x, axes, 0, 0, tiled=True)


def iota(shape, dim):
    return lax.broadcasted_iota(jnp.int32, shape, dim)


def call(kernel, shape, dtype, specs, flops=1 << 20, name=None):
    many = isinstance(shape, list)
    outs = [jax.ShapeDtypeStruct(s, d) for s, d in zip(shape, dtype)] if many else jax.ShapeDtypeStruct(shape, dtype)
    return pl.pallas_call(
        kernel,
        out_shape=outs,
        in_specs=specs,
        out_specs=[VMEM] * len(shape) if many else VMEM,
        compiler_params=pltpu.CompilerParams(vmem_limit_bytes=24 << 20),
        cost_estimate=pl.CostEstimate(flops=flops, bytes_accessed=1 << 20, transcendentals=0),
        name=name,
    )


def edges_kernel(key_ref, value_ref, core_ref, chip_ref):
    core = lax.axis_index("row_2")
    near = HALO * 16
    end = key_ref.shape[0] - near
    to_core = pl.multiple_of((1 - core) * end, near)
    to_chip = pl.multiple_of(core * end, near)
    for i, ref in enumerate((key_ref, value_ref)):
        core_ref[i] = ref[pl.ds(to_core, near), :]
        chip_ref[i] = ref[pl.ds(to_chip, near), :]


def attend_kernel(rows, cols, grid_rows, count_ref, reach_ref, q_ref, k_ref, v_ref, core_ref, chip_ref, target_ref, rate_ref, out_ref):
    core = lax.axis_index("row_2")
    base = lax.axis_index(ROW) * rows
    count = count_ref[0]
    tokens, near = rows * cols, HALO * cols
    span = tokens + 2 * near
    at = iota((1, span), 1)
    below, above = base + rows, base - HALO
    first_core = jnp.where(core == 0, below, above)
    first_chip = jnp.where(core == 0, above, below)
    start = jnp.where(at < tokens, base, jnp.where(at < tokens + near, first_core, first_chip))
    skip = jnp.where(at < tokens, 0, jnp.where(at < tokens + near, tokens, tokens + near))
    k_tok = start * cols + at - skip
    k_row = start + (at - skip) // cols
    q_at = iota((tokens, 1), 0)
    q_line = q_at // cols
    q_tok = base * cols + q_at
    reach = jnp.zeros((tokens, 1), jnp.int32)
    for r in range(rows):
        reach = jnp.where(q_line == r, reach_ref[r], reach)
    inside = (k_row >= 0) & (k_row < grid_rows)
    allowed = (jnp.abs(k_row - (base + q_line)) <= reach) & inside & ((k_tok < count) | (k_tok == q_tok))
    parts = []
    for h in range(q_ref.shape[1] // ATT_HD):
        lanes = slice(h * ATT_HD, (h + 1) * ATT_HD)
        keys = jnp.concatenate([k_ref[:, lanes], core_ref[0, :, lanes], chip_ref[0, :, lanes]], 0)
        values = jnp.concatenate([v_ref[:, lanes], core_ref[1, :, lanes], chip_ref[1, :, lanes]], 0)
        scores = dot(q_ref[:, lanes], keys, 1, 1) * (1.0 / math.sqrt(ATT_HD))
        scores = jnp.where(allowed, scores, -1e30)
        powers = jnp.exp(scores - jnp.max(scores, -1, keepdims=True))
        weights = (powers / jnp.sum(powers, -1, keepdims=True)).astype(BF)
        parts.append(dot(weights, values).astype(BF).astype(F32))
    attended = jnp.concatenate(parts, 1)
    mean = jnp.mean(attended * attended, -1, keepdims=True)
    out_ref[0] = (attended * lax.rsqrt(mean + 1e-06)).astype(BF)
    diagonal = iota((tokens, tokens), 0) == iota((tokens, tokens), 1)
    rates = jnp.sum(jnp.where(diagonal, rate_ref[...], 0.0), 1, keepdims=True)
    valid = jnp.where(q_tok < count, 1.0, 0.0)
    out_ref[1] = (rates * valid * target_ref[...].astype(F32)).astype(BF)


def grads_kernel(n_plane, n_view, own_ref, other_ref, w1_ref, w3_ref, w2_ref, out_ref, old_ref):
    core = lax.axis_index("row_2")
    half = HD // 2
    share = half // n_plane
    few = share // n_view
    keys = jnp.concatenate([own_ref[0], other_ref[0]], 0)
    scaled = jnp.concatenate([own_ref[1], other_ref[1]], 0)
    first = dot(keys, w1_ref[...])
    third = dot(keys, w3_ref[...])
    back = dot(scaled, w2_ref[...], 1, 1)
    sig = jax.nn.sigmoid(first)
    silu = first * sig
    gated = silu * third
    back_first = (back * third * (sig * (1.0 + first * (1.0 - sig)))).astype(BF)
    back_third = (back * silu).astype(BF)
    gated_half = jnp.where(core == 0, gated[:, :half], gated[:, half:]).astype(BF)
    lanes = pl.ds(pl.multiple_of(core * half, half), half)
    keys_half = jnp.concatenate([own_ref[0, :, lanes], other_ref[0, :, lanes]], 0)
    for k, (a, b) in enumerate(((keys_half, back_first), (keys_half, back_third), (gated_half, scaled))):
        g = dot(a, b, 0, 0).astype(BF)
        out_ref[:, k * share : (k + 1) * share, :] = g.reshape(n_plane, share, HD)
    base = pl.multiple_of(core * half + lax.axis_index(PLANE) * share, share)
    at = lax.axis_index("view") * few
    r, c = iota((8, share), 0), iota((8, share), 1)
    old = jnp.zeros((8, HD), F32)
    for k, ref in enumerate((w1_ref, w3_ref, w2_ref)):
        pick = (r - k * few >= 0) & (r - k * few < few) & (c == at + r - k * few)
        old += dot(jnp.where(pick, 1.0, 0.0).astype(BF), ref[pl.ds(base, share), :])
    old_ref[...] = old


def spread_kernel(n_view, few, count_ref, x_ref, out_ref):
    total = jnp.sum(x_ref[...].astype(F32), 0).astype(BF)
    lines = total.shape[0]
    share = lines // 3
    o, i = iota((n_view * 8, lines), 0), iota((n_view * 8, lines), 1)
    r = o % 8
    pick = (r < 3 * few) & (i == (r // few) * share + (o // 8) * few + r % few)
    moved = dot(jnp.where(pick, 1.0, 0.0).astype(BF), total)
    count = count_ref[0]
    lane = iota(moved.shape, 1)
    digits = jnp.where(lane == 0, count % 16, jnp.where(lane == 1, (count // 16) % 16, count // 256))
    moved = jnp.where(iota(moved.shape, 0) % 8 == 3 * few, digits.astype(F32), moved)
    out_ref[...] = moved.astype(BF).reshape(n_view, 8, HD)


def renew_kernel(few, x_ref, old_ref, out_ref):
    summed = jnp.sum(x_ref[...].astype(F32), 0)
    last = summed[3 * few : 3 * few + 1]
    total = last[:, 0:1] + 16.0 * last[:, 1:2] + 256.0 * last[:, 2:3]
    old = old_ref[...]
    raised = old + summed / total
    rescale = jnp.sqrt(jnp.sum(old * old, -1, keepdims=True) + 1e-06) / jnp.sqrt(
        jnp.sum(raised * raised, -1, keepdims=True) + 1e-06
    )
    new = (raised * rescale).astype(BF)
    out_ref[...] = jnp.broadcast_to(new[None], out_ref.shape)


def order_kernel(few, x_ref, out_ref):
    n_view = x_ref.shape[0]
    lines = out_ref.shape[1]
    share = lines // 3
    i, o = iota((lines, n_view * 8), 0), iota((lines, n_view * 8), 1)
    r = o % 8
    pick = (r < 3 * few) & (i == (r // few) * share + (o // 8) * few + r % few)
    moved = dot(jnp.where(pick, 1.0, 0.0).astype(BF), x_ref[...].reshape(n_view * 8, HD)).astype(BF)
    out_ref[...] = jnp.broadcast_to(moved[None], out_ref.shape)


def apply_kernel(own_ref, mine_ref, theirs_ref, out_ref):
    core = lax.axis_index("row_2")
    half = HD // 2
    share = mine_ref.shape[1] // 3

    def matrix(ref, k):
        return ref[:, k * share : (k + 1) * share, :].reshape(half, HD)

    k_mine = own_ref[0, :, pl.ds(pl.multiple_of(core * half, half), half)]
    k_theirs = own_ref[0, :, pl.ds(pl.multiple_of((1 - core) * half, half), half)]
    first = dot(k_mine, matrix(mine_ref, 0)) + dot(k_theirs, matrix(theirs_ref, 0))
    third = dot(k_mine, matrix(mine_ref, 1)) + dot(k_theirs, matrix(theirs_ref, 1))
    applied = (first * jax.nn.sigmoid(first) * third).astype(BF)
    left, right = applied[:, :half], applied[:, half:]
    a_mine = jnp.where(core == 0, left.astype(F32), right.astype(F32)).astype(BF)
    a_theirs = jnp.where(core == 0, right.astype(F32), left.astype(F32)).astype(BF)
    out_ref[...] = (dot(a_mine, matrix(mine_ref, 2)) + dot(a_theirs, matrix(theirs_ref, 2))).astype(BF)


def per_device(query_feats, key_feats, value_feats, target, token_rates, row_reach, view_counts, w_first, w_third, w_second):
    _, rows, cols, width = query_feats.shape
    tokens, near = rows * cols, HALO * cols
    n_row, n_plane, n_view = lax.axis_size(ROW), lax.axis_size(PLANE), lax.axis_size("view")
    share = HD // 2 // n_plane
    few = share // n_view
    flat = lambda x: x.reshape(tokens, width)

    edge = (2, near, width)
    to_core, to_chip = call(edges_kernel, [edge, edge], [BF, BF], [VMEM] * 2)(flat(key_feats), flat(value_feats))
    next_chip = [p for i in range(1, n_row - 1, 2) for p in ((i, i + 1), (i + 1, i))]
    from_core = lax.ppermute(to_core, "row_2", SWAP)
    from_chip = lax.ppermute(to_chip, ROW, next_chip)

    attend = lambda *refs: attend_kernel(rows, cols, n_row * rows, *refs)
    own = call(attend, (2, tokens, width), BF, [SMEM] * 2 + [VMEM] * 7)(
        view_counts, row_reach, flat(query_feats), flat(key_feats), flat(value_feats), from_core, from_chip, flat(target), token_rates[0]
    )
    other = lax.ppermute(own, "row_2", SWAP)
    grads, old = call(lambda *refs: grads_kernel(n_plane, n_view, *refs), [(n_plane, 3 * share, width), (8, width)], [BF, F32], [VMEM] * 5)(
        own, other, w_first[0], w_third[0], w_second[0]
    )
    part = exchange(grads, PLANE)
    part = call(lambda *refs: spread_kernel(n_view, few, *refs), (n_view, 8, width), BF, [SMEM, VMEM])(view_counts, part)
    part = exchange(part, "view")
    new = call(lambda *refs: renew_kernel(few, *refs), (n_view, 8, width), BF, [VMEM] * 2)(part, old)
    new = exchange(new, "view")
    lines = call(lambda *refs: order_kernel(few, *refs), (n_plane, 3 * share, width), BF, [VMEM])(new)
    mine = exchange(lines, PLANE)
    theirs = lax.ppermute(mine, "row_2", SWAP)
    out = call(apply_kernel, (tokens, width), BF, [VMEM] * 3)(own, mine, theirs)
    return out.reshape(1, rows, cols, width)


def solution(mesh):
    torus = Mesh(
        mesh.devices.reshape(mesh.shape["head"], mesh.shape["view"], 2, 4, 2),
        ("head", "view", "row_0", "row_1", "row_2"),
    )
    feats = P("view", ROW, None, "head")
    heads = P("head", None, None)
    return jax.shard_map(
        per_device,
        mesh=torus,
        in_specs=(feats, feats, feats, feats, P("view", "head", ROW), P(ROW), P("view"), heads, heads, heads),
        out_specs=feats,
        check_vma=False,
    )
```

```python
import math

import jax
import jax.numpy as jnp
from jax import lax
from jax.experimental import pallas as pl
from jax.experimental.pallas import tpu as pltpu
from jax.sharding import Mesh
from jax.sharding import PartitionSpec as P

HD = 512
ATT_HD = 128
HALO = 2
PLANE = ("row_0", "row_1")
ROW = ("row_0", "row_1", "row_2")
SWAP = [(0, 1), (1, 0)]
BF = jnp.bfloat16
F32 = jnp.float32
VMEM = pl.BlockSpec(memory_space=pltpu.VMEM)
SMEM = pl.BlockSpec(memory_space=pltpu.SMEM)
HBM = pl.BlockSpec(memory_space=pltpu.HBM)


def dot(a, b, ca=1, cb=0):
    return lax.dot_general(a, b, (((ca,), (cb,)), ((), ())), preferred_element_type=F32)


def exchange(x, axes):
    return lax.all_to_all(x, axes, 0, 0, tiled=True)


def iota(shape, dim):
    return lax.broadcasted_iota(jnp.int32, shape, dim)


def call(kernel, shapes, specs, copies=0):
    many = isinstance(shapes, list)
    outs = [jax.ShapeDtypeStruct(*s) for s in shapes] if many else jax.ShapeDtypeStruct(*shapes)
    return pl.pallas_call(
        kernel,
        out_shape=outs,
        in_specs=specs,
        out_specs=[VMEM] * len(shapes) if many else VMEM,
        scratch_shapes=[pltpu.SemaphoreType.DMA((copies,))] if copies else [],
        compiler_params=pltpu.CompilerParams(vmem_limit_bytes=24 << 20),
        cost_estimate=pl.CostEstimate(flops=1 << 20, bytes_accessed=1 << 20, transcendentals=0),
    )


def edges_kernel(q_in, k_in, v_in, t_in, q_ref, k_ref, v_ref, t_ref, core_ref, chip_ref, sems):
    core = lax.axis_index("row_2")
    near = HALO * 16
    end = k_in.shape[0] - near
    to_core = pl.ds(pl.multiple_of((1 - core) * end, near), near)
    to_chip = pl.ds(pl.multiple_of(core * end, near), near)
    pairs = []
    for i, ref in enumerate((k_in, v_in)):
        pairs += [(ref.at[to_core], core_ref.at[i]), (ref.at[to_chip], chip_ref.at[i])]
    pairs += [(k_in, k_ref), (v_in, v_ref), (q_in, q_ref), (t_in, t_ref)]
    copies = [pltpu.make_async_copy(a, b, sems.at[n]) for n, (a, b) in enumerate(pairs)]
    for c in copies:
        c.start()
    for c in copies:
        c.wait()


def attend_kernel(rows, cols, grid_rows, count_ref, reach_ref, q_ref, k_ref, v_ref, core_ref, chip_ref, target_ref, rate_ref, w1_in, w3_in, w2_in, out_ref, w1_ref, w3_ref, w2_ref, sems):
    copies = [
        pltpu.make_async_copy(a, b, sems.at[n])
        for n, (a, b) in enumerate(((w1_in, w1_ref), (w3_in, w3_ref), (w2_in, w2_ref)))
    ]
    for c in copies:
        c.start()
    core = lax.axis_index("row_2")
    base = lax.axis_index(ROW) * rows
    count = count_ref[0]
    tokens, near = rows * cols, HALO * cols
    span = tokens + 2 * near
    at = iota((1, span), 1)
    below, above = base + rows, base - HALO
    first_core = jnp.where(core == 0, below, above)
    first_chip = jnp.where(core == 0, above, below)
    start = jnp.where(at < tokens, base, jnp.where(at < tokens + near, first_core, first_chip))
    skip = jnp.where(at < tokens, 0, jnp.where(at < tokens + near, tokens, tokens + near))
    k_tok = start * cols + at - skip
    k_row = start + (at - skip) // cols
    q_at = iota((tokens, 1), 0)
    q_line = q_at // cols
    q_tok = base * cols + q_at
    reach = jnp.zeros((tokens, 1), jnp.int32)
    for r in range(rows):
        reach = jnp.where(q_line == r, reach_ref[r], reach)
    inside = (k_row >= 0) & (k_row < grid_rows)
    allowed = (jnp.abs(k_row - (base + q_line)) <= reach) & inside & ((k_tok < count) | (k_tok == q_tok))
    parts = []
    for h in range(q_ref.shape[1] // ATT_HD):
        lanes = slice(h * ATT_HD, (h + 1) * ATT_HD)
        keys = jnp.concatenate([k_ref[:, lanes], core_ref[0, :, lanes], chip_ref[0, :, lanes]], 0)
        values = jnp.concatenate([v_ref[:, lanes], core_ref[1, :, lanes], chip_ref[1, :, lanes]], 0)
        scores = dot(q_ref[:, lanes], keys, 1, 1) * (1.0 / math.sqrt(ATT_HD))
        scores = jnp.where(allowed, scores, -1e30)
        powers = jnp.exp(scores - jnp.max(scores, -1, keepdims=True))
        weights = (powers / jnp.sum(powers, -1, keepdims=True)).astype(BF)
        parts.append(dot(weights, values).astype(BF).astype(F32))
    attended = jnp.concatenate(parts, 1)
    mean = jnp.mean(attended * attended, -1, keepdims=True)
    out_ref[0] = (attended * lax.rsqrt(mean + 1e-06)).astype(BF)
    diagonal = iota((tokens, tokens), 0) == iota((tokens, tokens), 1)
    rates = jnp.sum(jnp.where(diagonal, rate_ref[...], 0.0), 1, keepdims=True)
    valid = jnp.where(q_tok < count, 1.0, 0.0)
    out_ref[1] = (rates * valid * target_ref[...].astype(F32)).astype(BF)
    for c in copies:
        c.wait()


def grads_kernel(n_plane, n_near, own_ref, other_ref, w1_ref, w3_ref, w2_ref, out_ref, old_ref):
    core = lax.axis_index("row_2")
    half = HD // 2
    share = half // n_plane
    few = share // n_near
    keys = jnp.concatenate([own_ref[0], other_ref[0]], 0)
    scaled = jnp.concatenate([own_ref[1], other_ref[1]], 0)
    first = dot(keys, w1_ref[...])
    third = dot(keys, w3_ref[...])
    back = dot(scaled, w2_ref[...], 1, 1)
    sig = jax.nn.sigmoid(first)
    silu = first * sig
    gated = silu * third
    back_first = (back * third * (sig * (1.0 + first * (1.0 - sig)))).astype(BF)
    back_third = (back * silu).astype(BF)
    gated_half = jnp.where(core == 0, gated[:, :half], gated[:, half:]).astype(BF)
    lanes = pl.ds(pl.multiple_of(core * half, half), half)
    keys_half = jnp.concatenate([own_ref[0, :, lanes], other_ref[0, :, lanes]], 0)
    for k, (a, b) in enumerate(((keys_half, back_first), (keys_half, back_third), (gated_half, scaled))):
        g = dot(a, b, 0, 0).astype(BF)
        out_ref[:, k * share : (k + 1) * share, :] = g.reshape(n_plane, share, HD)
    base = pl.multiple_of(core * half + lax.axis_index(PLANE) * share, share)
    at = lax.axis_index("near") * few
    pick = jnp.where(iota((few, share), 1) == at + iota((few, share), 0), 1.0, 0.0).astype(BF)
    for k, ref in enumerate((w1_ref, w3_ref, w2_ref)):
        old_ref[:, k * HD : (k + 1) * HD] = dot(pick, ref[pl.ds(base, share), :])


def spread_kernel(n_near, few, count_ref, x_ref, out_ref):
    total = jnp.sum(x_ref[...].astype(F32), 0)
    share = total.shape[0] // 3
    for k in range(3):
        for u in range(n_near):
            at = k * share + u * few
            out_ref[u, :, k * HD : (k + 1) * HD] = total[at : at + few].astype(BF)
    count = count_ref[0]
    lane = iota((few, 128), 1)
    digits = jnp.where(lane == 0, count % 16, jnp.where(lane == 1, (count // 16) % 16, count // 256))
    digits = digits.astype(F32).astype(BF)
    for u in range(n_near):
        out_ref[u, :, 3 * HD :] = digits


def gather_kernel(x_ref, out_ref):
    total = jnp.sum(x_ref[...].astype(F32), 0).astype(BF)
    out_ref[...] = jnp.broadcast_to(total[None], out_ref.shape)


def renew_kernel(x_ref, old_ref, out_ref):
    summed = jnp.sum(x_ref[...].astype(F32), 0)
    last = summed[0:1, 3 * HD :]
    total = last[:, 0:1] + 16.0 * last[:, 1:2] + 256.0 * last[:, 2:3]
    for k in range(3):
        lanes = slice(k * HD, (k + 1) * HD)
        old = old_ref[:, lanes]
        raised = old + summed[:, lanes] / total
        rescale = jnp.sqrt(jnp.sum(old * old, -1, keepdims=True) + 1e-06) / jnp.sqrt(
            jnp.sum(raised * raised, -1, keepdims=True) + 1e-06
        )
        new = (raised * rescale).astype(BF)
        for u in range(out_ref.shape[0]):
            out_ref[u, :, lanes] = new


def order_kernel(x_ref, out_ref):
    n_near = x_ref.shape[0]
    x = x_ref[...].astype(F32)
    lines = jnp.concatenate([x[u, :, k * HD : (k + 1) * HD] for k in range(3) for u in range(n_near)], 0).astype(BF)
    out_ref[...] = jnp.broadcast_to(lines[None], out_ref.shape)


def apply_kernel(own_ref, mine_ref, theirs_ref, out_ref):
    core = lax.axis_index("row_2")
    half = HD // 2
    share = mine_ref.shape[1] // 3

    def matrix(ref, k):
        return ref[:, k * share : (k + 1) * share, :].reshape(half, HD)

    k_mine = own_ref[0, :, pl.ds(pl.multiple_of(core * half, half), half)]
    k_theirs = own_ref[0, :, pl.ds(pl.multiple_of((1 - core) * half, half), half)]
    first = dot(k_mine, matrix(mine_ref, 0)) + dot(k_theirs, matrix(theirs_ref, 0))
    third = dot(k_mine, matrix(mine_ref, 1)) + dot(k_theirs, matrix(theirs_ref, 1))
    applied = (first * jax.nn.sigmoid(first) * third).astype(BF)
    left, right = applied[:, :half], applied[:, half:]
    a_mine = jnp.where(core == 0, left.astype(F32), right.astype(F32)).astype(BF)
    a_theirs = jnp.where(core == 0, right.astype(F32), left.astype(F32)).astype(BF)
    out_ref[...] = (dot(a_mine, matrix(mine_ref, 2)) + dot(a_theirs, matrix(theirs_ref, 2))).astype(BF)


def per_device(query_feats, key_feats, value_feats, target, token_rates, row_reach, view_counts, w_first, w_third, w_second):
    _, rows, cols, width = query_feats.shape
    tokens, near = rows * cols, HALO * cols
    n_row, n_plane, n_near, n_far = (lax.axis_size(axes) for axes in (ROW, PLANE, "near", "far"))
    share = HD // 2 // n_plane
    few = share // n_near
    flat = lambda x: x.reshape(tokens, width)
    in_hbm = lambda x: pltpu.with_memory_space_constraint(x, pltpu.HBM)

    block, edge, matrix = ((tokens, width), BF), ((2, near, width), BF), ((HD, HD), BF)
    query, key, value, aim, to_core, to_chip = call(edges_kernel, [block] * 4 + [edge] * 2, [HBM] * 4, 8)(
        *(in_hbm(flat(x)) for x in (query_feats, key_feats, value_feats, target))
    )
    next_chip = [p for i in range(1, n_row - 1, 2) for p in ((i, i + 1), (i + 1, i))]
    from_core = lax.ppermute(to_core, "row_2", SWAP)
    from_chip = lax.ppermute(to_chip, ROW, next_chip)

    attend = lambda *refs: attend_kernel(rows, cols, n_row * rows, *refs)
    own, w1, w3, w2 = call(attend, [((2, tokens, width), BF)] + [matrix] * 3, [SMEM] * 2 + [VMEM] * 7 + [HBM] * 3, 3)(
        view_counts, row_reach, query, key, value, from_core, from_chip, aim, token_rates[0], *(in_hbm(w[0]) for w in (w_first, w_third, w_second))
    )
    other = lax.ppermute(own, "row_2", SWAP)
    grads = lambda *refs: grads_kernel(n_plane, n_near, *refs)
    part, old = call(grads, [((n_plane, 3 * share, width), BF), ((few, 3 * width), F32)], [VMEM] * 5)(own, other, w1, w3, w2)
    part = exchange(part, PLANE)
    spread = lambda *refs: spread_kernel(n_near, few, *refs)
    part = call(spread, ((n_near, few, 3 * width + 128), BF), [SMEM, VMEM])(view_counts, part)
    part = exchange(part, "near")
    part = call(gather_kernel, ((n_far, few, 3 * width + 128), BF), [VMEM])(part)
    part = exchange(part, "far")
    new = call(renew_kernel, ((n_near, few, 3 * width), BF), [VMEM] * 2)(part, old)
    new = exchange(new, "near")
    lines = call(order_kernel, ((n_plane, 3 * share, width), BF), [VMEM])(new)
    mine = exchange(lines, PLANE)
    theirs = lax.ppermute(mine, "row_2", SWAP)
    out = call(apply_kernel, ((tokens, width), BF), [VMEM] * 3)(own, mine, theirs)
    return out.reshape(1, rows, cols, width)


def solution(mesh):
    torus = Mesh(
        mesh.devices.reshape(mesh.shape["head"], mesh.shape["view"] // 4, 4, 2, 4, 2),
        ("head", "far", "near", "row_0", "row_1", "row_2"),
    )
    views = ("far", "near")
    feats = P(views, ROW, None, "head")
    heads = P("head", None, None)
    return jax.shard_map(
        per_device,
        mesh=torus,
        in_specs=(feats, feats, feats, feats, P(views, "head", ROW), P(ROW), P(views), heads, heads, heads),
        out_specs=feats,
        check_vma=False,
    )
```

```python
import math

import jax
import jax.numpy as jnp
from jax import lax
from jax.experimental import pallas as pl
from jax.experimental.pallas import tpu as pltpu
from jax.sharding import Mesh
from jax.sharding import PartitionSpec as P

HD = 512
ATT_HD = 128
HALO = 2
PLANE = ("row_0", "row_1")
ROW = ("row_0", "row_1", "row_2")
SWAP = [(0, 1), (1, 0)]
BF = jnp.bfloat16
F32 = jnp.float32
VMEM = pl.BlockSpec(memory_space=pltpu.VMEM)
SMEM = pl.BlockSpec(memory_space=pltpu.SMEM)
HBM = pl.BlockSpec(memory_space=pltpu.HBM)


def dot(a, b, ca=1, cb=0):
    return lax.dot_general(a, b, (((ca,), (cb,)), ((), ())), preferred_element_type=F32)


def exchange(x, axes):
    return lax.all_to_all(x, axes, 0, 0, tiled=True)


def iota(shape, dim):
    return lax.broadcasted_iota(jnp.int32, shape, dim)


def call(kernel, shapes, specs, copies=0):
    many = isinstance(shapes, list)
    outs = [jax.ShapeDtypeStruct(*s) for s in shapes] if many else jax.ShapeDtypeStruct(*shapes)
    return pl.pallas_call(
        kernel,
        out_shape=outs,
        in_specs=specs,
        out_specs=[VMEM] * len(shapes) if many else VMEM,
        scratch_shapes=[pltpu.SemaphoreType.DMA((copies,))] if copies else [],
        compiler_params=pltpu.CompilerParams(vmem_limit_bytes=24 << 20),
        cost_estimate=pl.CostEstimate(flops=1 << 20, bytes_accessed=1 << 20, transcendentals=0),
    )


def start_all(pairs, sems):
    copies = [pltpu.make_async_copy(a, b, sems.at[n]) for n, (a, b) in enumerate(pairs)]
    for c in copies:
        c.start()
    return copies


def edges_kernel(k_in, v_in, core_ref, chip_ref, sems):
    core = lax.axis_index("row_2")
    near = HALO * 16
    end = k_in.shape[0] - near
    to_core = pl.ds(pl.multiple_of((1 - core) * end, near), near)
    to_chip = pl.ds(pl.multiple_of(core * end, near), near)
    pairs = []
    for i, ref in enumerate((k_in, v_in)):
        pairs += [(ref.at[to_core], core_ref.at[i]), (ref.at[to_chip], chip_ref.at[i])]
    for c in start_all(pairs, sems):
        c.wait()


def prepare_kernel(rows, cols, count_ref, edge_ref, rate_ref, q_in, k_in, v_in, t_in, q_ref, k_ref, v_ref, scaled_ref, t_ref, sems):
    copies = start_all([(t_in, t_ref), (q_in, q_ref), (k_in, k_ref), (v_in, v_ref)], sems)
    tokens = rows * cols
    diagonal = iota((tokens, tokens), 0) == iota((tokens, tokens), 1)
    rates = jnp.sum(jnp.where(diagonal, rate_ref[...], 0.0), 1, keepdims=True)
    q_tok = lax.axis_index(ROW) * tokens + iota((tokens, 1), 0)
    valid = jnp.where(q_tok < count_ref[0], 1.0, 0.0)
    copies[0].wait()
    scaled_ref[...] = (rates * valid * t_ref[...].astype(F32)).astype(BF)
    for c in copies[1:]:
        c.wait()


def attend_kernel(rows, cols, grid_rows, count_ref, reach_ref, q_ref, k_ref, v_ref, core_ref, chip_ref, scaled_ref, out_ref):
    core = lax.axis_index("row_2")
    base = lax.axis_index(ROW) * rows
    count = count_ref[0]
    tokens, near = rows * cols, HALO * cols
    span = tokens + 2 * near
    at = iota((1, span), 1)
    below, above = base + rows, base - HALO
    first_core = jnp.where(core == 0, below, above)
    first_chip = jnp.where(core == 0, above, below)
    start = jnp.where(at < tokens, base, jnp.where(at < tokens + near, first_core, first_chip))
    skip = jnp.where(at < tokens, 0, jnp.where(at < tokens + near, tokens, tokens + near))
    k_tok = start * cols + at - skip
    k_row = start + (at - skip) // cols
    q_at = iota((tokens, 1), 0)
    q_line = q_at // cols
    q_tok = base * cols + q_at
    reach = jnp.zeros((tokens, 1), jnp.int32)
    for r in range(rows):
        reach = jnp.where(q_line == r, reach_ref[r], reach)
    inside = (k_row >= 0) & (k_row < grid_rows)
    allowed = (jnp.abs(k_row - (base + q_line)) <= reach) & inside & ((k_tok < count) | (k_tok == q_tok))
    parts = []
    for h in range(q_ref.shape[1] // ATT_HD):
        lanes = slice(h * ATT_HD, (h + 1) * ATT_HD)
        keys = jnp.concatenate([k_ref[:, lanes], core_ref[0, :, lanes], chip_ref[0, :, lanes]], 0)
        values = jnp.concatenate([v_ref[:, lanes], core_ref[1, :, lanes], chip_ref[1, :, lanes]], 0)
        scores = dot(q_ref[:, lanes], keys, 1, 1) * (1.0 / math.sqrt(ATT_HD))
        scores = jnp.where(allowed, scores, -1e30)
        powers = jnp.exp(scores - jnp.max(scores, -1, keepdims=True))
        weights = (powers / jnp.sum(powers, -1, keepdims=True)).astype(BF)
        parts.append(dot(weights, values).astype(BF).astype(F32))
    attended = jnp.concatenate(parts, 1)
    mean = jnp.mean(attended * attended, -1, keepdims=True)
    out_ref[0] = (attended * lax.rsqrt(mean + 1e-06)).astype(BF)
    out_ref[1] = scaled_ref[...]


def forward(keys, scaled, w1_ref, w3_ref, w2_ref):
    first = dot(keys, w1_ref[...])
    third = dot(keys, w3_ref[...])
    back = dot(scaled, w2_ref[...], 1, 1)
    sig = jax.nn.sigmoid(first)
    silu = first * sig
    back_first = back * third * (sig * (1.0 + first * (1.0 - sig)))
    return back_first.astype(BF), (back * silu).astype(BF), silu * third


def own_half(x, core):
    half = x.shape[1] // 2
    return jnp.where(core == 0, x[:, :half], x[:, half:])


def forward_kernel(n_plane, n_near, own_ref, w1_ref, w3_ref, w2_ref, out_ref, gated_ref, old_ref):
    core = lax.axis_index("row_2")
    half = HD // 2
    share = half // n_plane
    few = share // n_near
    back_first, back_third, gated = forward(own_ref[0], own_ref[1], w1_ref, w3_ref, w2_ref)
    out_ref[0] = back_first
    out_ref[1] = back_third
    gated_ref[...] = own_half(gated, core).astype(BF)
    base = pl.multiple_of(core * half + lax.axis_index(PLANE) * share, share)
    at = lax.axis_index("near") * few
    pick = jnp.where(iota((few, share), 1) == at + iota((few, share), 0), 1.0, 0.0).astype(BF)
    for k, ref in enumerate((w1_ref, w3_ref, w2_ref)):
        old_ref[:, k * HD : (k + 1) * HD] = dot(pick, ref[pl.ds(base, share), :])


def grads_kernel(n_plane, own_ref, mine_ref, mine_gated_ref, other_ref, w1_ref, w3_ref, w2_ref, out_ref):
    core = lax.axis_index("row_2")
    half = HD // 2
    share = half // n_plane
    back_first, back_third, gated = forward(other_ref[0], other_ref[1], w1_ref, w3_ref, w2_ref)
    lanes = pl.ds(pl.multiple_of(core * half, half), half)
    both = lambda a, b: jnp.concatenate([a, b], 0)
    keys = both(own_ref[0, :, lanes], other_ref[0, :, lanes])
    gated = both(mine_gated_ref[...], own_half(gated, core).astype(BF))
    pairs = (
        (keys, both(mine_ref[0], back_first)),
        (keys, both(mine_ref[1], back_third)),
        (gated, both(own_ref[1], other_ref[1])),
    )
    for k, (a, b) in enumerate(pairs):
        g = dot(a, b, 0, 0).astype(BF)
        out_ref[:, k * share : (k + 1) * share, :] = g.reshape(n_plane, share, HD)


def spread_kernel(n_near, few, count_ref, x_ref, out_ref):
    total = jnp.sum(x_ref[...].astype(F32), 0)
    share = total.shape[0] // 3
    for k in range(3):
        for u in range(n_near):
            at = k * share + u * few
            out_ref[u, :, k * HD : (k + 1) * HD] = total[at : at + few].astype(BF)
    count = count_ref[0]
    lane = iota((few, 128), 1)
    digits = jnp.where(lane == 0, count % 16, jnp.where(lane == 1, (count // 16) % 16, count // 256))
    digits = digits.astype(F32).astype(BF)
    for u in range(n_near):
        out_ref[u, :, 3 * HD :] = digits


def gather_kernel(x_ref, out_ref):
    total = jnp.sum(x_ref[...].astype(F32), 0).astype(BF)
    out_ref[...] = jnp.broadcast_to(total[None], out_ref.shape)


def renew_kernel(x_ref, old_ref, out_ref):
    summed = jnp.sum(x_ref[...].astype(F32), 0)
    last = summed[0:1, 3 * HD :]
    total = last[:, 0:1] + 16.0 * last[:, 1:2] + 256.0 * last[:, 2:3]
    for k in range(3):
        lanes = slice(k * HD, (k + 1) * HD)
        old = old_ref[:, lanes]
        raised = old + summed[:, lanes] / total
        rescale = jnp.sqrt(jnp.sum(old * old, -1, keepdims=True) + 1e-06) / jnp.sqrt(
            jnp.sum(raised * raised, -1, keepdims=True) + 1e-06
        )
        new = (raised * rescale).astype(BF)
        for u in range(out_ref.shape[0]):
            out_ref[u, :, lanes] = new


def order_kernel(x_ref, out_ref):
    n_near = x_ref.shape[0]
    x = x_ref[...].astype(F32)
    lines = jnp.concatenate([x[u, :, k * HD : (k + 1) * HD] for k in range(3) for u in range(n_near)], 0).astype(BF)
    out_ref[...] = jnp.broadcast_to(lines[None], out_ref.shape)


def matrix(ref, k):
    share = ref.shape[1] // 3
    return ref[:, k * share : (k + 1) * share, :].reshape(ref.shape[0] * share, HD)


def half_kernel(own_ref, mine_ref, out_ref):
    half = HD // 2
    keys = own_ref[0, :, pl.ds(pl.multiple_of(lax.axis_index("row_2") * half, half), half)]
    out_ref[0] = dot(keys, matrix(mine_ref, 0))
    out_ref[1] = dot(keys, matrix(mine_ref, 1))


def apply_kernel(own_ref, part_ref, mine_ref, theirs_ref, out_ref):
    core = lax.axis_index("row_2")
    half = HD // 2
    keys = own_ref[0, :, pl.ds(pl.multiple_of((1 - core) * half, half), half)]
    first = part_ref[0] + dot(keys, matrix(theirs_ref, 0))
    third = part_ref[1] + dot(keys, matrix(theirs_ref, 1))
    applied = first * jax.nn.sigmoid(first) * third
    a_mine, a_theirs = own_half(applied, core).astype(BF), own_half(applied, 1 - core).astype(BF)
    out_ref[...] = (dot(a_mine, matrix(mine_ref, 2)) + dot(a_theirs, matrix(theirs_ref, 2))).astype(BF)


def per_device(query_feats, key_feats, value_feats, target, token_rates, row_reach, view_counts, w_first, w_third, w_second):
    _, rows, cols, width = query_feats.shape
    tokens, near = rows * cols, HALO * cols
    n_row, n_plane, n_near, n_far = (lax.axis_size(axes) for axes in (ROW, PLANE, "near", "far"))
    share = HD // 2 // n_plane
    few = share // n_near
    flat = lambda x: x.reshape(tokens, width)
    in_hbm = lambda x: pltpu.with_memory_space_constraint(x, pltpu.HBM)

    block, edge = ((tokens, width), BF), ((2, near, width), BF)
    query, key, value, aim = (in_hbm(flat(x)) for x in (query_feats, key_feats, value_feats, target))
    to_core, to_chip = call(edges_kernel, [edge] * 2, [HBM] * 2, 4)(key, value)
    next_chip = [p for i in range(1, n_row - 1, 2) for p in ((i, i + 1), (i + 1, i))]
    from_chip = lax.ppermute(to_chip, ROW, next_chip)
    from_core = lax.ppermute(to_core, "row_2", SWAP)

    prepare = lambda *refs: prepare_kernel(rows, cols, *refs)
    query, key, value, scaled, _ = call(prepare, [block] * 5, [SMEM] + [VMEM] * 2 + [HBM] * 4, 4)(
        view_counts, to_core, token_rates[0], query, key, value, aim
    )
    attend = lambda *refs: attend_kernel(rows, cols, n_row * rows, *refs)
    own = call(attend, ((2, tokens, width), BF), [SMEM] * 2 + [VMEM] * 6)(
        view_counts, row_reach, query, key, value, from_core, from_chip, scaled
    )
    other = lax.ppermute(own, "row_2", SWAP)
    ws = w_first[0], w_third[0], w_second[0]
    ahead = lambda *refs: forward_kernel(n_plane, n_near, *refs)
    back, gated, old = call(ahead, [((2, tokens, width), BF), ((tokens, width // 2), BF), ((few, 3 * width), F32)], [VMEM] * 4)(own, *ws)
    grads = lambda *refs: grads_kernel(n_plane, *refs)
    part = call(grads, ((n_plane, 3 * share, width), BF), [VMEM] * 7)(own, back, gated, other, *ws)
    part = exchange(part, PLANE)
    spread = lambda *refs: spread_kernel(n_near, few, *refs)
    part = call(spread, ((n_near, few, 3 * width + 128), BF), [SMEM, VMEM])(view_counts, part)
    part = exchange(part, "near")
    part = call(gather_kernel, ((n_far, few, 3 * width + 128), BF), [VMEM])(part)
    part = exchange(part, "far")
    new = call(renew_kernel, ((n_near, few, 3 * width), BF), [VMEM] * 2)(part, old)
    new = exchange(new, "near")
    lines = call(order_kernel, ((n_plane, 3 * share, width), BF), [VMEM])(new)
    mine = exchange(lines, PLANE)
    theirs = lax.ppermute(mine, "row_2", SWAP)
    part = call(half_kernel, ((2, tokens, width), F32), [VMEM] * 2)(own, mine)
    out = call(apply_kernel, ((tokens, width), BF), [VMEM] * 4)(own, part, mine, theirs)
    return out.reshape(1, rows, cols, width)


def solution(mesh):
    torus = Mesh(
        mesh.devices.reshape(mesh.shape["head"], mesh.shape["view"] // 4, 4, 2, 4, 2),
        ("head", "far", "near", "row_0", "row_1", "row_2"),
    )
    views = ("far", "near")
    feats = P(views, ROW, None, "head")
    heads = P("head", None, None)
    return jax.shard_map(
        per_device,
        mesh=torus,
        in_specs=(feats, feats, feats, feats, P(views, "head", ROW), P(ROW), P(views), heads, heads, heads),
        out_specs=feats,
        check_vma=False,
    )
```

```python
import math

import jax
import jax.numpy as jnp
from jax import lax
from jax.experimental import pallas as pl
from jax.experimental.pallas import tpu as pltpu
from jax.sharding import Mesh
from jax.sharding import PartitionSpec as P

HD = 512
ATT_HD = 128
HALO = 2
PLANE = ("row_0", "row_1")
ROW = ("row_0", "row_1", "row_2")
SWAP = [(0, 1), (1, 0)]
BF = jnp.bfloat16
F32 = jnp.float32
VMEM = pl.BlockSpec(memory_space=pltpu.VMEM)
SMEM = pl.BlockSpec(memory_space=pltpu.SMEM)
HBM = pl.BlockSpec(memory_space=pltpu.HBM)


def dot(a, b, ca=1, cb=0):
    return lax.dot_general(a, b, (((ca,), (cb,)), ((), ())), preferred_element_type=F32)


def exchange(x, axes):
    return lax.all_to_all(x, axes, 0, 0, tiled=True)


def iota(shape, dim):
    return lax.broadcasted_iota(jnp.int32, shape, dim)


def call(kernel, shapes, specs, copies=0):
    many = isinstance(shapes, list)
    outs = [jax.ShapeDtypeStruct(*s) for s in shapes] if many else jax.ShapeDtypeStruct(*shapes)
    return pl.pallas_call(
        kernel,
        out_shape=outs,
        in_specs=specs,
        out_specs=[VMEM] * len(shapes) if many else VMEM,
        scratch_shapes=[pltpu.SemaphoreType.DMA((copies,))] if copies else [],
        compiler_params=pltpu.CompilerParams(vmem_limit_bytes=24 << 20),
        cost_estimate=pl.CostEstimate(flops=1 << 20, bytes_accessed=1 << 20, transcendentals=0),
    )


def start_all(pairs, sems):
    copies = [pltpu.make_async_copy(a, b, sems.at[n]) for n, (a, b) in enumerate(pairs)]
    for c in copies:
        c.start()
    return copies


def edges_kernel(q_in, k_in, v_in, t_in, r_in, core_ref, chip_ref, q_ref, k_ref, v_ref, t_ref, r_ref, sems):
    core = lax.axis_index("row_2")
    near = HALO * 16
    end = k_in.shape[0] - near
    to_core = pl.ds(pl.multiple_of((1 - core) * end, near), near)
    to_chip = pl.ds(pl.multiple_of(core * end, near), near)
    pairs = []
    for i, ref in enumerate((k_in, v_in)):
        pairs += [(ref.at[to_core], core_ref.at[i]), (ref.at[to_chip], chip_ref.at[i])]
    for c in start_all(pairs + [(r_in, r_ref), (t_in, t_ref), (q_in, q_ref), (k_in, k_ref), (v_in, v_ref)], sems):
        c.wait()


def scale_kernel(tokens, count_ref, edge_ref, rate_ref, t_ref, out_ref):
    diagonal = iota((tokens, tokens), 0) == iota((tokens, tokens), 1)
    q_tok = lax.axis_index(ROW) * tokens + iota((1, tokens), 1)
    valid = jnp.where(q_tok < count_ref[0], 1.0, 0.0)
    rates = jnp.sum(jnp.where(diagonal, rate_ref[...] * valid, 0.0), 1, keepdims=True)
    out_ref[...] = (rates * t_ref[...].astype(F32)).astype(BF)


def attend_kernel(rows, cols, grid_rows, count_ref, reach_ref, q_ref, k_ref, v_ref, core_ref, chip_ref, scaled_ref, out_ref):
    core = lax.axis_index("row_2")
    base = lax.axis_index(ROW) * rows
    count = count_ref[0]
    tokens, near = rows * cols, HALO * cols
    span = tokens + 2 * near
    at = iota((span, 1), 0)
    below, above = base + rows, base - HALO
    first_core = jnp.where(core == 0, below, above)
    first_chip = jnp.where(core == 0, above, below)
    start = jnp.where(at < tokens, base, jnp.where(at < tokens + near, first_core, first_chip))
    skip = jnp.where(at < tokens, 0, jnp.where(at < tokens + near, tokens, tokens + near))
    k_tok = start * cols + at - skip
    k_row = start + (at - skip) // cols
    q_at = iota((1, tokens), 1)
    q_line = q_at // cols
    q_tok = base * cols + q_at
    reach = jnp.zeros((1, tokens), jnp.int32)
    for r in range(rows):
        reach = jnp.where(q_line == r, reach_ref[r], reach)
    valid = (k_tok < count) & (k_row >= 0) & (k_row < grid_rows)
    k_row = jnp.where(valid, k_row, -(1 << 20))
    allowed = (jnp.abs(k_row - (base + q_line)) <= reach) | (k_tok == q_tok)
    parts = []
    for h in range(q_ref.shape[1] // ATT_HD):
        lanes = slice(h * ATT_HD, (h + 1) * ATT_HD)
        keys = jnp.concatenate([k_ref[:, lanes], core_ref[0, :, lanes], chip_ref[0, :, lanes]], 0)
        values = jnp.concatenate([v_ref[:, lanes], core_ref[1, :, lanes], chip_ref[1, :, lanes]], 0)
        scores = jnp.where(allowed, dot(keys, q_ref[:, lanes], 1, 1), -1e30)
        powers = jnp.exp2((scores - jnp.max(scores, 0, keepdims=True)) * (math.log2(math.e) / math.sqrt(ATT_HD)))
        weights = (powers * (1.0 / jnp.sum(powers, 0, keepdims=True))).astype(BF)
        parts.append(dot(weights, values, 0, 0).astype(BF).astype(F32))
    attended = jnp.concatenate(parts, 1)
    mean = jnp.mean(attended * attended, -1, keepdims=True)
    out_ref[0] = (attended * lax.rsqrt(mean + 1e-06)).astype(BF)
    out_ref[1] = scaled_ref[...]


def forward(keys, scaled, w1_ref, w3_ref, w2_ref):
    first = dot(keys, w1_ref[...])
    third = dot(keys, w3_ref[...])
    back = dot(scaled, w2_ref[...], 1, 1)
    sig = jax.nn.sigmoid(first)
    silu = first * sig
    back_first = back * third * (sig * (1.0 + first * (1.0 - sig)))
    return back_first.astype(BF), (back * silu).astype(BF), silu * third


def own_half(x, core):
    half = x.shape[1] // 2
    return jnp.where(core == 0, x[:, :half], x[:, half:])


def forward_kernel(n_plane, n_near, own_ref, w1_ref, w3_ref, w2_ref, out_ref, gated_ref, old_ref):
    core = lax.axis_index("row_2")
    half = HD // 2
    share = half // n_plane
    few = share // n_near
    back_first, back_third, gated = forward(own_ref[0], own_ref[1], w1_ref, w3_ref, w2_ref)
    out_ref[0] = back_first
    out_ref[1] = back_third
    gated_ref[...] = own_half(gated, core).astype(BF)
    base = pl.multiple_of(core * half + lax.axis_index(PLANE) * share, share)
    at = lax.axis_index("near") * few
    pick = jnp.where(iota((few, share), 1) == at + iota((few, share), 0), 1.0, 0.0).astype(BF)
    for k, ref in enumerate((w1_ref, w3_ref, w2_ref)):
        old_ref[:, k * HD : (k + 1) * HD] = dot(pick, ref[pl.ds(base, share), :])


def grads_kernel(n_plane, own_ref, mine_ref, mine_gated_ref, other_ref, w1_ref, w3_ref, w2_ref, out_ref):
    core = lax.axis_index("row_2")
    half = HD // 2
    share = half // n_plane
    back_first, back_third, gated = forward(other_ref[0], other_ref[1], w1_ref, w3_ref, w2_ref)
    lanes = pl.ds(pl.multiple_of(core * half, half), half)
    both = lambda a, b: jnp.concatenate([a, b], 0)
    keys = both(own_ref[0, :, lanes], other_ref[0, :, lanes])
    gated = both(mine_gated_ref[...], own_half(gated, core).astype(BF))
    pairs = (
        (keys, both(mine_ref[0], back_first)),
        (keys, both(mine_ref[1], back_third)),
        (gated, both(own_ref[1], other_ref[1])),
    )
    for k, (a, b) in enumerate(pairs):
        g = dot(a, b, 0, 0).astype(BF)
        out_ref[:, k * share : (k + 1) * share, :] = g.reshape(n_plane, share, HD)


def spread_kernel(n_near, few, count_ref, x_ref, out_ref):
    total = jnp.sum(x_ref[...].astype(F32), 0)
    share = total.shape[0] // 3
    for k in range(3):
        for u in range(n_near):
            at = k * share + u * few
            out_ref[u, :, k * HD : (k + 1) * HD] = total[at : at + few].astype(BF)
    count = count_ref[0]
    lane = iota((few, 128), 1)
    digits = jnp.where(lane == 0, count % 16, jnp.where(lane == 1, (count // 16) % 16, count // 256))
    digits = digits.astype(F32).astype(BF)
    for u in range(n_near):
        out_ref[u, :, 3 * HD :] = digits


def gather_kernel(x_ref, out_ref):
    total = jnp.sum(x_ref[...].astype(F32), 0).astype(BF)
    out_ref[...] = jnp.broadcast_to(total[None], out_ref.shape)


def renew_kernel(x_ref, old_ref, out_ref):
    summed = jnp.sum(x_ref[...].astype(F32), 0)
    last = summed[0:1, 3 * HD :]
    total = last[:, 0:1] + 16.0 * last[:, 1:2] + 256.0 * last[:, 2:3]
    for k in range(3):
        lanes = slice(k * HD, (k + 1) * HD)
        old = old_ref[:, lanes]
        raised = old + summed[:, lanes] / total
        rescale = jnp.sqrt(jnp.sum(old * old, -1, keepdims=True) + 1e-06) / jnp.sqrt(
            jnp.sum(raised * raised, -1, keepdims=True) + 1e-06
        )
        new = (raised * rescale).astype(BF)
        for u in range(out_ref.shape[0]):
            out_ref[u, :, lanes] = new


def order_kernel(x_ref, out_ref):
    n_near = x_ref.shape[0]
    x = x_ref[...].astype(F32)
    lines = jnp.concatenate([x[u, :, k * HD : (k + 1) * HD] for k in range(3) for u in range(n_near)], 0).astype(BF)
    out_ref[...] = jnp.broadcast_to(lines[None], out_ref.shape)


def matrix(ref, k):
    share = ref.shape[1] // 3
    return ref[:, k * share : (k + 1) * share, :].reshape(ref.shape[0] * share, HD)


def half_kernel(own_ref, mine_ref, out_ref):
    half = HD // 2
    keys = own_ref[0, :, pl.ds(pl.multiple_of(lax.axis_index("row_2") * half, half), half)]
    out_ref[0] = dot(keys, matrix(mine_ref, 0))
    out_ref[1] = dot(keys, matrix(mine_ref, 1))


def apply_kernel(own_ref, part_ref, mine_ref, theirs_ref, out_ref):
    core = lax.axis_index("row_2")
    half = HD // 2
    keys = own_ref[0, :, pl.ds(pl.multiple_of((1 - core) * half, half), half)]
    first = part_ref[0] + dot(keys, matrix(theirs_ref, 0))
    third = part_ref[1] + dot(keys, matrix(theirs_ref, 1))
    applied = first * jax.nn.sigmoid(first) * third
    a_mine, a_theirs = own_half(applied, core).astype(BF), own_half(applied, 1 - core).astype(BF)
    out_ref[...] = (dot(a_mine, matrix(mine_ref, 2)) + dot(a_theirs, matrix(theirs_ref, 2))).astype(BF)


def per_device(query_feats, key_feats, value_feats, target, token_rates, row_reach, view_counts, w_first, w_third, w_second):
    _, rows, cols, width = query_feats.shape
    tokens, near = rows * cols, HALO * cols
    n_row, n_plane, n_near, n_far = (lax.axis_size(axes) for axes in (ROW, PLANE, "near", "far"))
    share = HD // 2 // n_plane
    few = share // n_near
    flat = lambda x: x.reshape(tokens, width)
    in_hbm = lambda x: pltpu.with_memory_space_constraint(x, pltpu.HBM)

    block, edge = ((tokens, width), BF), ((2, near, width), BF)
    query, key, value, aim = (in_hbm(flat(x)) for x in (query_feats, key_feats, value_feats, target))
    to_core, to_chip, query, key, value, aim, rates = call(edges_kernel, [edge] * 2 + [block] * 4 + [((1, tokens), F32)], [HBM] * 5, 9)(
        query, key, value, aim, in_hbm(token_rates[0])
    )
    next_chip = [p for i in range(1, n_row - 1, 2) for p in ((i, i + 1), (i + 1, i))]
    from_chip = lax.ppermute(to_chip, ROW, next_chip)
    from_core = lax.ppermute(to_core, "row_2", SWAP)

    scaled = call(lambda *refs: scale_kernel(tokens, *refs), block, [SMEM] + [VMEM] * 3)(view_counts, to_core, rates, aim)
    attend = lambda *refs: attend_kernel(rows, cols, n_row * rows, *refs)
    own = call(attend, ((2, tokens, width), BF), [SMEM] * 2 + [VMEM] * 6)(
        view_counts, row_reach, query, key, value, from_core, from_chip, scaled
    )
    other = lax.ppermute(own, "row_2", SWAP)
    ws = w_first[0], w_third[0], w_second[0]
    ahead = lambda *refs: forward_kernel(n_plane, n_near, *refs)
    back, gated, old = call(ahead, [((2, tokens, width), BF), ((tokens, width // 2), BF), ((few, 3 * width), F32)], [VMEM] * 4)(own, *ws)
    grads = lambda *refs: grads_kernel(n_plane, *refs)
    part = call(grads, ((n_plane, 3 * share, width), BF), [VMEM] * 7)(own, back, gated, other, *ws)
    part = exchange(part, PLANE)
    spread = lambda *refs: spread_kernel(n_near, few, *refs)
    part = call(spread, ((n_near, few, 3 * width + 128), BF), [SMEM, VMEM])(view_counts, part)
    part = exchange(part, "near")
    part = call(gather_kernel, ((n_far, few, 3 * width + 128), BF), [VMEM])(part)
    part = exchange(part, "far")
    new = call(renew_kernel, ((n_near, few, 3 * width), BF), [VMEM] * 2)(part, old)
    new = exchange(new, "near")
    lines = call(order_kernel, ((n_plane, 3 * share, width), BF), [VMEM])(new)
    mine = exchange(lines, PLANE)
    theirs = lax.ppermute(mine, "row_2", SWAP)
    part = call(half_kernel, ((2, tokens, width), F32), [VMEM] * 2)(own, mine)
    out = call(apply_kernel, ((tokens, width), BF), [VMEM] * 4)(own, part, mine, theirs)
    return out.reshape(1, rows, cols, width)


def solution(mesh):
    torus = Mesh(
        mesh.devices.reshape(mesh.shape["head"], mesh.shape["view"] // 4, 4, 2, 4, 2),
        ("head", "far", "near", "row_0", "row_1", "row_2"),
    )
    views = ("far", "near")
    feats = P(views, ROW, None, "head")
    heads = P("head", None, None)
    return jax.shard_map(
        per_device,
        mesh=torus,
        in_specs=(feats, feats, feats, feats, P(views, "head", ROW), P(ROW), P(views), heads, heads, heads),
        out_specs=feats,
        check_vma=False,
    )
```

```python
import math

import jax
import jax.numpy as jnp
from jax import lax
from jax.experimental import pallas as pl
from jax.experimental.pallas import tpu as pltpu
from jax.sharding import Mesh
from jax.sharding import PartitionSpec as P

HD = 512
ATT_HD = 128
HALO = 2
PLANE = ("row_0", "row_1")
ROW = ("row_0", "row_1", "row_2")
SWAP = [(0, 1), (1, 0)]
BF = jnp.bfloat16
F32 = jnp.float32
VMEM = pl.BlockSpec(memory_space=pltpu.VMEM)
SMEM = pl.BlockSpec(memory_space=pltpu.SMEM)
HBM = pl.BlockSpec(memory_space=pltpu.HBM)


def dot(a, b, ca=1, cb=0):
    return lax.dot_general(a, b, (((ca,), (cb,)), ((), ())), preferred_element_type=F32)


def exchange(x, axes):
    return lax.all_to_all(x, axes, 0, 0, tiled=True)


def iota(shape, dim):
    return lax.broadcasted_iota(jnp.int32, shape, dim)


def call(kernel, shapes, specs, scratch=(), out=VMEM):
    many = isinstance(shapes, list)
    outs = [jax.ShapeDtypeStruct(*s) for s in shapes] if many else jax.ShapeDtypeStruct(*shapes)
    return pl.pallas_call(
        kernel,
        out_shape=outs,
        in_specs=specs,
        out_specs=[out] * len(shapes) if many else out,
        scratch_shapes=scratch,
        compiler_params=pltpu.CompilerParams(vmem_limit_bytes=24 << 20),
        cost_estimate=pl.CostEstimate(flops=1 << 20, bytes_accessed=1 << 20, transcendentals=0),
    )


def start_all(pairs, sems):
    copies = [pltpu.make_async_copy(a, b, sems.at[n]) for n, (a, b) in enumerate(pairs)]
    for c in copies:
        c.start()
    return copies


def edges_kernel(
    cols, q_in, k_in, v_in, t_in, rate_in, reach_in, core_ref, chip_ref, q_ref, k_ref, v_ref, t_ref, rate_ref, reach_ref, sems, reach_smem
):
    core = lax.axis_index("row_2")
    near = HALO * cols
    end = k_in.shape[0] - near
    to_core = pl.ds(pl.multiple_of((1 - core) * end, near), near)
    to_chip = pl.ds(pl.multiple_of(core * end, near), near)
    pairs = [(reach_in, reach_smem)]
    for i, ref in enumerate((k_in, v_in)):
        pairs += [(ref.at[to_core], core_ref.at[i]), (ref.at[to_chip], chip_ref.at[i])]
    pairs += [(rate_in, rate_ref), (t_in, t_ref), (q_in, q_ref), (k_in, k_ref), (v_in, v_ref)]
    copies = start_all(pairs, sems)
    copies[0].wait()
    line = iota(reach_ref.shape, 1) // cols
    reach = jnp.zeros(reach_ref.shape, jnp.int32)
    for r in range(reach_smem.shape[0]):
        reach = jnp.where(line == r, reach_smem[r], reach)
    reach_ref[...] = reach
    for c in copies[1:]:
        c.wait()


def scale_kernel(tokens, count_ref, edge_ref, rate_ref, t_ref, out_ref):
    diagonal = iota((tokens, tokens), 0) == iota((tokens, tokens), 1)
    q_tok = lax.axis_index(ROW) * tokens + iota((1, tokens), 1)
    valid = jnp.where(q_tok < count_ref[0], 1.0, 0.0)
    rates = jnp.sum(jnp.where(diagonal, rate_ref[...] * valid, 0.0), 1, keepdims=True)
    out_ref[...] = (rates * t_ref[...].astype(F32)).astype(BF)


def attend_kernel(rows, cols, grid_rows, count_ref, reach_ref, q_ref, k_ref, v_ref, core_ref, chip_ref, scaled_ref, out_ref):
    core = lax.axis_index("row_2")
    base = lax.axis_index(ROW) * rows
    tokens, near = rows * cols, HALO * cols
    span = tokens + 2 * near
    at = iota((span, 1), 0)
    below, above = base + rows, base - HALO
    first_core = jnp.where(core == 0, below, above)
    first_chip = jnp.where(core == 0, above, below)
    start = jnp.where(at < tokens, base, jnp.where(at < tokens + near, first_core, first_chip))
    skip = jnp.where(at < tokens, 0, jnp.where(at < tokens + near, tokens, tokens + near))
    k_tok = start * cols + at - skip
    k_row = start + (at - skip) // cols
    q_at = iota((1, tokens), 1)
    q_row = base + q_at // cols
    q_tok = base * cols + q_at
    valid = (k_tok < count_ref[0]) & (k_row >= 0) & (k_row < grid_rows)
    k_row = jnp.where(valid, k_row, -(1 << 20))
    allowed = (jnp.abs(k_row - q_row) <= reach_ref[...]) | (k_tok == q_tok)
    heads = [slice(at, at + ATT_HD) for at in range(0, q_ref.shape[1], ATT_HD)]
    factor = math.log2(math.e) / math.sqrt(ATT_HD)
    keys = [jnp.concatenate([k_ref[:, h], core_ref[0, :, h], chip_ref[0, :, h]], 0) for h in heads]
    values = [jnp.concatenate([v_ref[:, h], core_ref[1, :, h], chip_ref[1, :, h]], 0) for h in heads]
    scores = [jnp.where(allowed, dot(k, q_ref[:, h], 1, 1), -1e30) for k, h in zip(keys, heads)]
    tops = [jnp.max(s, 0, keepdims=True) for s in scores]
    powers = [jnp.exp2((s - t) * factor) for s, t in zip(scores, tops)]
    sums = [jnp.sum(p, 0, keepdims=True) for p in powers]
    weights = [(p * (1.0 / s)).astype(BF) for p, s in zip(powers, sums)]
    attended = [dot(w, v, 0, 0).astype(BF).astype(F32) for w, v in zip(weights, values)]
    mean = sum(jnp.sum(a * a, -1, keepdims=True) for a in attended) / q_ref.shape[1]
    inverse = lax.rsqrt(mean + 1e-06)
    for a, h in zip(attended, heads):
        out_ref[0, :, h] = (a * inverse).astype(BF)
    out_ref[1] = scaled_ref[...]


def forward(keys, scaled, w1_ref, w3_ref, w2_ref):
    first = dot(keys, w1_ref[...])
    third = dot(keys, w3_ref[...])
    back = dot(scaled, w2_ref[...], 1, 1)
    sig = jax.nn.sigmoid(first)
    silu = first * sig
    back_first = back * third * (sig * (1.0 + first * (1.0 - sig)))
    return back_first.astype(BF), (back * silu).astype(BF), silu * third


def own_half(x, core):
    half = x.shape[1] // 2
    return jnp.where(core == 0, x[:, :half], x[:, half:])


def forward_kernel(n_plane, n_near, own_ref, w1_ref, w3_ref, w2_ref, out_ref, gated_ref, old_ref):
    core = lax.axis_index("row_2")
    half = HD // 2
    share = half // n_plane
    few = share // n_near
    back_first, back_third, gated = forward(own_ref[0], own_ref[1], w1_ref, w3_ref, w2_ref)
    out_ref[0] = back_first
    out_ref[1] = back_third
    gated_ref[...] = own_half(gated, core).astype(BF)
    base = pl.multiple_of(core * half + lax.axis_index(PLANE) * share, share)
    at = lax.axis_index("near") * few
    pick = jnp.where(iota((few, share), 1) == at + iota((few, share), 0), 1.0, 0.0).astype(BF)
    for k, ref in enumerate((w1_ref, w3_ref, w2_ref)):
        old_ref[:, k * HD : (k + 1) * HD] = dot(pick, ref[pl.ds(base, share), :])


def grads_kernel(n_plane, own_ref, mine_ref, mine_gated_ref, other_ref, w1_ref, w3_ref, w2_ref, out_ref):
    core = lax.axis_index("row_2")
    half = HD // 2
    share = half // n_plane
    back_first, back_third, gated = forward(other_ref[0], other_ref[1], w1_ref, w3_ref, w2_ref)
    lanes = pl.ds(pl.multiple_of(core * half, half), half)
    both = lambda a, b: jnp.concatenate([a, b], 0)
    keys = both(own_ref[0, :, lanes], other_ref[0, :, lanes])
    gated = both(mine_gated_ref[...], own_half(gated, core).astype(BF))
    pairs = (
        (keys, both(mine_ref[0], back_first)),
        (keys, both(mine_ref[1], back_third)),
        (gated, both(own_ref[1], other_ref[1])),
    )
    for k, (a, b) in enumerate(pairs):
        g = dot(a, b, 0, 0).astype(BF)
        out_ref[:, k * share : (k + 1) * share, :] = g.reshape(n_plane, share, HD)


def spread_kernel(n_near, few, count_ref, x_ref, out_ref):
    total = jnp.sum(x_ref[...].astype(F32), 0)
    share = total.shape[0] // 3
    for k in range(3):
        for u in range(n_near):
            at = k * share + u * few
            out_ref[u, :, k * HD : (k + 1) * HD] = total[at : at + few].astype(BF)
    count = count_ref[0]
    lane = iota((few, 128), 1)
    digits = jnp.where(lane == 0, count % 16, jnp.where(lane == 1, (count // 16) % 16, count // 256))
    digits = digits.astype(F32).astype(BF)
    for u in range(n_near):
        out_ref[u, :, 3 * HD :] = digits


def gather_kernel(x_ref, out_ref):
    total = jnp.sum(x_ref[...].astype(F32), 0).astype(BF)
    out_ref[...] = jnp.broadcast_to(total[None], out_ref.shape)


def renew_kernel(x_ref, old_ref, out_ref):
    summed = jnp.sum(x_ref[...].astype(F32), 0)
    last = summed[0:1, 3 * HD :]
    total = last[:, 0:1] + 16.0 * last[:, 1:2] + 256.0 * last[:, 2:3]
    for k in range(3):
        lanes = slice(k * HD, (k + 1) * HD)
        old = old_ref[:, lanes]
        raised = old + summed[:, lanes] / total
        rescale = jnp.sqrt(jnp.sum(old * old, -1, keepdims=True) + 1e-06) / jnp.sqrt(
            jnp.sum(raised * raised, -1, keepdims=True) + 1e-06
        )
        new = (raised * rescale).astype(BF)
        for u in range(out_ref.shape[0]):
            out_ref[u, :, lanes] = new


def order_kernel(x_ref, out_ref):
    n_near = x_ref.shape[0]
    x = x_ref[...].astype(F32)
    lines = jnp.concatenate([x[u, :, k * HD : (k + 1) * HD] for k in range(3) for u in range(n_near)], 0).astype(BF)
    out_ref[...] = jnp.broadcast_to(lines[None], out_ref.shape)


def matrix(ref, k):
    share = ref.shape[1] // 3
    return ref[:, k * share : (k + 1) * share, :].reshape(ref.shape[0] * share, HD)


def half_kernel(own_ref, mine_ref, out_ref):
    half = HD // 2
    keys = own_ref[0, :, pl.ds(pl.multiple_of(lax.axis_index("row_2") * half, half), half)]
    out_ref[0] = dot(keys, matrix(mine_ref, 0))
    out_ref[1] = dot(keys, matrix(mine_ref, 1))


def apply_kernel(own_ref, part_ref, mine_ref, theirs_ref, out_hbm, out_ref, sems):
    core = lax.axis_index("row_2")
    half = HD // 2
    keys = own_ref[0, :, pl.ds(pl.multiple_of((1 - core) * half, half), half)]
    first = part_ref[0] + dot(keys, matrix(theirs_ref, 0))
    third = part_ref[1] + dot(keys, matrix(theirs_ref, 1))
    applied = first * jax.nn.sigmoid(first) * third
    a_mine, a_theirs = own_half(applied, core).astype(BF), own_half(applied, 1 - core).astype(BF)
    rows = out_ref.shape[0] // 2
    copies = []
    for n in range(2):
        lines = slice(n * rows, (n + 1) * rows)
        out_ref[lines, :] = (dot(a_mine[lines], matrix(mine_ref, 2)) + dot(a_theirs[lines], matrix(theirs_ref, 2))).astype(BF)
        at = pl.ds(n * rows, rows)
        copies.append(pltpu.make_async_copy(out_ref.at[at], out_hbm.at[at], sems.at[n]))
        copies[n].start()
    for c in copies:
        c.wait()


def per_device(query_feats, key_feats, value_feats, target, token_rates, row_reach, view_counts, w_first, w_third, w_second):
    _, rows, cols, width = query_feats.shape
    tokens, near = rows * cols, HALO * cols
    n_row, n_plane, n_near, n_far = (lax.axis_size(axes) for axes in (ROW, PLANE, "near", "far"))
    share = HD // 2 // n_plane
    few = share // n_near
    flat = lambda x: x.reshape(tokens, width)
    in_hbm = lambda x: pltpu.with_memory_space_constraint(x, pltpu.HBM)

    block, edge = ((tokens, width), BF), ((2, near, width), BF)
    query, key, value, aim = (in_hbm(flat(x)) for x in (query_feats, key_feats, value_feats, target))
    row_of = lambda dtype: ((1, tokens), dtype)
    to_core, to_chip, query, key, value, aim, rates, reach = call(
        lambda *refs: edges_kernel(cols, *refs),
        [edge] * 2 + [block] * 4 + [row_of(F32), row_of(jnp.int32)],
        [HBM] * 6,
        [pltpu.SemaphoreType.DMA((10,)), pltpu.SMEM(row_reach.shape, jnp.int32)],
    )(query, key, value, aim, in_hbm(token_rates[0]), in_hbm(row_reach))
    next_chip = [p for i in range(1, n_row - 1, 2) for p in ((i, i + 1), (i + 1, i))]
    from_chip = lax.ppermute(to_chip, ROW, next_chip)
    from_core = lax.ppermute(to_core, "row_2", SWAP)

    scaled = call(lambda *refs: scale_kernel(tokens, *refs), block, [SMEM] + [VMEM] * 3)(view_counts, to_core, rates, aim)
    attend = lambda *refs: attend_kernel(rows, cols, n_row * rows, *refs)
    own = call(attend, ((2, tokens, width), BF), [SMEM] + [VMEM] * 7)(
        view_counts, reach, query, key, value, from_core, from_chip, scaled
    )
    other = lax.ppermute(own, "row_2", SWAP)
    ws = w_first[0], w_third[0], w_second[0]
    ahead = lambda *refs: forward_kernel(n_plane, n_near, *refs)
    back, gated, old = call(ahead, [((2, tokens, width), BF), ((tokens, width // 2), BF), ((few, 3 * width), F32)], [VMEM] * 4)(own, *ws)
    grads = lambda *refs: grads_kernel(n_plane, *refs)
    part = call(grads, ((n_plane, 3 * share, width), BF), [VMEM] * 7)(own, back, gated, other, *ws)
    part = exchange(part, PLANE)
    spread = lambda *refs: spread_kernel(n_near, few, *refs)
    part = call(spread, ((n_near, few, 3 * width + 128), BF), [SMEM, VMEM])(view_counts, part)
    part = exchange(part, "near")
    part = call(gather_kernel, ((n_far, few, 3 * width + 128), BF), [VMEM])(part)
    part = exchange(part, "far")
    new = call(renew_kernel, ((n_near, few, 3 * width), BF), [VMEM] * 2)(part, old)
    new = exchange(new, "near")
    lines = call(order_kernel, ((n_plane, 3 * share, width), BF), [VMEM])(new)
    mine = exchange(lines, PLANE)
    theirs = lax.ppermute(mine, "row_2", SWAP)
    part = call(half_kernel, ((2, tokens, width), F32), [VMEM] * 2)(own, mine)
    scratch = [pltpu.VMEM((tokens, width), BF), pltpu.SemaphoreType.DMA((2,))]
    out = call(apply_kernel, block, [VMEM] * 4, scratch, HBM)(own, part, mine, theirs)
    return out.reshape(1, rows, cols, width)


def solution(mesh):
    torus = Mesh(
        mesh.devices.reshape(mesh.shape["head"], mesh.shape["view"] // 4, 4, 2, 4, 2),
        ("head", "far", "near", "row_0", "row_1", "row_2"),
    )
    views = ("far", "near")
    feats = P(views, ROW, None, "head")
    heads = P("head", None, None)
    return jax.shard_map(
        per_device,
        mesh=torus,
        in_specs=(feats, feats, feats, feats, P(views, "head", ROW), P(ROW), P(views), heads, heads, heads),
        out_specs=feats,
        check_vma=False,
    )
```

```python
import math

import jax
import jax.numpy as jnp
from jax import lax
from jax.experimental import pallas as pl
from jax.experimental.pallas import tpu as pltpu
from jax.sharding import Mesh
from jax.sharding import PartitionSpec as P

HD = 512
ATT_HD = 128
HALO = 2
PLANE = ("row_0", "row_1")
ROW = ("row_0", "row_1", "row_2")
SWAP = [(0, 1), (1, 0)]
BF = jnp.bfloat16
F32 = jnp.float32
VMEM = pl.BlockSpec(memory_space=pltpu.VMEM)
SMEM = pl.BlockSpec(memory_space=pltpu.SMEM)
HBM = pl.BlockSpec(memory_space=pltpu.HBM)


def dot(a, b, ca=1, cb=0):
    return lax.dot_general(a, b, (((ca,), (cb,)), ((), ())), preferred_element_type=F32)


def exchange(x, axes):
    return lax.all_to_all(x, axes, 0, 0, tiled=True)


def iota(shape, dim):
    return lax.broadcasted_iota(jnp.int32, shape, dim)


def call(kernel, shapes, specs, scratch=(), out=VMEM):
    many = isinstance(shapes, list)
    outs = [jax.ShapeDtypeStruct(*s) for s in shapes] if many else jax.ShapeDtypeStruct(*shapes)
    return pl.pallas_call(
        kernel,
        out_shape=outs,
        in_specs=specs,
        out_specs=[out] * len(shapes) if many else out,
        scratch_shapes=scratch,
        compiler_params=pltpu.CompilerParams(vmem_limit_bytes=24 << 20),
        cost_estimate=pl.CostEstimate(flops=1 << 20, bytes_accessed=1 << 20, transcendentals=0),
    )


def start_all(pairs, sems):
    copies = [pltpu.make_async_copy(a, b, sems.at[n]) for n, (a, b) in enumerate(pairs)]
    for c in copies:
        c.start()
    return copies


def edges_kernel(
    cols, q_in, k_in, v_in, t_in, rate_in, reach_in, core_ref, chip_ref, q_ref, k_ref, v_ref, t_ref, rate_ref, reach_ref, sems, reach_smem
):
    core = lax.axis_index("row_2")
    near = HALO * cols
    end = k_in.shape[0] - near
    to_core = pl.ds(pl.multiple_of((1 - core) * end, near), near)
    to_chip = pl.ds(pl.multiple_of(core * end, near), near)
    pairs = [(reach_in, reach_smem)]
    for i, ref in enumerate((k_in, v_in)):
        pairs += [(ref.at[to_core], core_ref.at[i]), (ref.at[to_chip], chip_ref.at[i])]
    pairs += [(rate_in, rate_ref), (t_in, t_ref), (q_in, q_ref), (k_in, k_ref), (v_in, v_ref)]
    copies = start_all(pairs, sems)
    copies[0].wait()
    line = iota(reach_ref.shape, 1) // cols
    reach = jnp.zeros(reach_ref.shape, jnp.int32)
    for r in range(reach_smem.shape[0]):
        reach = jnp.where(line == r, reach_smem[r], reach)
    reach_ref[...] = reach
    for c in copies[1:]:
        c.wait()


def scale_kernel(tokens, count_ref, edge_ref, rate_ref, t_ref, out_ref):
    diagonal = iota((tokens, tokens), 0) == iota((tokens, tokens), 1)
    q_tok = lax.axis_index(ROW) * tokens + iota((1, tokens), 1)
    valid = jnp.where(q_tok < count_ref[0], 1.0, 0.0)
    rates = jnp.sum(jnp.where(diagonal, rate_ref[...] * valid, 0.0), 1, keepdims=True)
    out_ref[...] = (rates * t_ref[...].astype(F32)).astype(BF)


def attend_kernel(rows, cols, grid_rows, count_ref, reach_ref, q_ref, k_ref, v_ref, core_ref, chip_ref, scaled_ref, out_ref):
    core = lax.axis_index("row_2")
    base = lax.axis_index(ROW) * rows
    tokens, near = rows * cols, HALO * cols
    span = tokens + 2 * near
    at = iota((span, 1), 0)
    below, above = base + rows, base - HALO
    first_core = jnp.where(core == 0, below, above)
    first_chip = jnp.where(core == 0, above, below)
    start = jnp.where(at < tokens, base, jnp.where(at < tokens + near, first_core, first_chip))
    skip = jnp.where(at < tokens, 0, jnp.where(at < tokens + near, tokens, tokens + near))
    k_tok = start * cols + at - skip
    k_row = start + (at - skip) // cols
    q_at = iota((1, tokens), 1)
    q_row = base + q_at // cols
    q_tok = base * cols + q_at
    valid = (k_tok < count_ref[0]) & (k_row >= 0) & (k_row < grid_rows)
    k_row = jnp.where(valid, k_row, -(1 << 20))
    allowed = (jnp.abs(k_row - q_row) <= reach_ref[...]) | (k_tok == q_tok)
    heads = [slice(at, at + ATT_HD) for at in range(0, q_ref.shape[1], ATT_HD)]
    factor = math.log2(math.e) / math.sqrt(ATT_HD)
    keys = [jnp.concatenate([k_ref[:, h], core_ref[0, :, h], chip_ref[0, :, h]], 0) for h in heads]
    values = [jnp.concatenate([v_ref[:, h], core_ref[1, :, h], chip_ref[1, :, h]], 0) for h in heads]
    scores = [jnp.where(allowed, dot(k, q_ref[:, h], 1, 1), -1e30) for k, h in zip(keys, heads)]
    tops = [jnp.max(s, 0, keepdims=True) for s in scores]
    powers = [jnp.exp2((s - t) * factor) for s, t in zip(scores, tops)]
    sums = [jnp.sum(p, 0, keepdims=True) for p in powers]
    weights = [(p * (1.0 / s)).astype(BF) for p, s in zip(powers, sums)]
    attended = [dot(w, v, 0, 0).astype(BF).astype(F32) for w, v in zip(weights, values)]
    mean = sum(jnp.sum(a * a, -1, keepdims=True) for a in attended) / q_ref.shape[1]
    inverse = lax.rsqrt(mean + 1e-06)
    for a, h in zip(attended, heads):
        out_ref[0, :, h] = (a * inverse).astype(BF)
    out_ref[1] = scaled_ref[...]


def forward(keys, scaled, w1_ref, w3_ref, w2_ref):
    first = dot(keys, w1_ref[...])
    third = dot(keys, w3_ref[...])
    back = dot(scaled, w2_ref[...], 1, 1)
    sig = jax.nn.sigmoid(first)
    silu = first * sig
    back_first = back * third * (sig * (1.0 + first * (1.0 - sig)))
    return back_first.astype(BF), (back * silu).astype(BF), silu * third


def own_half(x, core):
    half = x.shape[1] // 2
    return jnp.where(core == 0, x[:, :half], x[:, half:])


def forward_kernel(n_plane, n_near, own_ref, w1_ref, w3_ref, w2_ref, out_ref, gated_ref, old_ref):
    core = lax.axis_index("row_2")
    half = HD // 2
    share = half // n_plane
    few = share // n_near
    back_first, back_third, gated = forward(own_ref[0], own_ref[1], w1_ref, w3_ref, w2_ref)
    out_ref[0] = back_first
    out_ref[1] = back_third
    gated_ref[...] = own_half(gated, core).astype(BF)
    base = pl.multiple_of(core * half + lax.axis_index(PLANE) * share, share)
    at = lax.axis_index("near") * few
    pick = jnp.where(iota((few, share), 1) == at + iota((few, share), 0), 1.0, 0.0).astype(BF)
    for k, ref in enumerate((w1_ref, w3_ref, w2_ref)):
        old_ref[:, k * HD : (k + 1) * HD] = dot(pick, ref[pl.ds(base, share), :])


def grads_kernel(n_plane, own_ref, mine_ref, mine_gated_ref, other_ref, w1_ref, w3_ref, w2_ref, out_ref):
    core = lax.axis_index("row_2")
    half = HD // 2
    share = half // n_plane
    back_first, back_third, gated = forward(other_ref[0], other_ref[1], w1_ref, w3_ref, w2_ref)
    lanes = pl.ds(pl.multiple_of(core * half, half), half)
    both = lambda a, b: jnp.concatenate([a, b], 0)
    keys = both(own_ref[0, :, lanes], other_ref[0, :, lanes])
    gated = both(mine_gated_ref[...], own_half(gated, core).astype(BF))
    pairs = (
        (keys, both(mine_ref[0], back_first)),
        (keys, both(mine_ref[1], back_third)),
        (gated, both(own_ref[1], other_ref[1])),
    )
    for k, (a, b) in enumerate(pairs):
        g = dot(a, b, 0, 0).astype(BF)
        out_ref[:, k * share : (k + 1) * share, :] = g.reshape(n_plane, share, HD)


def spread_kernel(n_near, few, count_ref, x_ref, out_ref):
    total = jnp.sum(x_ref[...].astype(F32), 0)
    share = total.shape[0] // 3
    for k in range(3):
        for u in range(n_near):
            at = k * share + u * few
            out_ref[u, :, k * HD : (k + 1) * HD] = total[at : at + few].astype(BF)
    count = count_ref[0]
    lane = iota((few, 128), 1)
    digits = jnp.where(lane == 0, count % 16, jnp.where(lane == 1, (count // 16) % 16, count // 256))
    digits = digits.astype(F32).astype(BF)
    for u in range(n_near):
        out_ref[u, :, 3 * HD :] = digits


def gather_kernel(x_ref, out_ref):
    total = jnp.sum(x_ref[...].astype(F32), 0).astype(BF)
    out_ref[...] = jnp.broadcast_to(total[None], out_ref.shape)


def renew_kernel(x_ref, old_ref, out_ref):
    summed = jnp.sum(x_ref[...].astype(F32), 0)
    last = summed[0:1, 3 * HD :]
    total = last[:, 0:1] + 16.0 * last[:, 1:2] + 256.0 * last[:, 2:3]
    for k in range(3):
        lanes = slice(k * HD, (k + 1) * HD)
        old = old_ref[:, lanes]
        raised = old + summed[:, lanes] / total
        rescale = jnp.sqrt(jnp.sum(old * old, -1, keepdims=True) + 1e-06) / jnp.sqrt(
            jnp.sum(raised * raised, -1, keepdims=True) + 1e-06
        )
        new = (raised * rescale).astype(BF)
        for u in range(out_ref.shape[0]):
            out_ref[u, :, lanes] = new


def order_kernel(x_ref, out_ref):
    n_near = x_ref.shape[0]
    x = x_ref[...].astype(F32)
    lines = jnp.concatenate([x[u, :, k * HD : (k + 1) * HD] for k in range(3) for u in range(n_near)], 0).astype(BF)
    out_ref[...] = jnp.broadcast_to(lines[None], out_ref.shape)


def matrix(ref, k):
    share = ref.shape[1] // 3
    return ref[:, k * share : (k + 1) * share, :].reshape(ref.shape[0] * share, HD)


def half_kernel(own_ref, mine_ref, out_ref):
    half = HD // 2
    keys = own_ref[0, :, pl.ds(pl.multiple_of(lax.axis_index("row_2") * half, half), half)]
    out_ref[0] = dot(keys, matrix(mine_ref, 0))
    out_ref[1] = dot(keys, matrix(mine_ref, 1))


def apply_kernel(own_ref, part_ref, mine_ref, theirs_ref, out_hbm, out_ref, sems):
    core = lax.axis_index("row_2")
    half = HD // 2
    keys = own_ref[0, :, pl.ds(pl.multiple_of((1 - core) * half, half), half)]
    first = part_ref[0] + dot(keys, matrix(theirs_ref, 0))
    third = part_ref[1] + dot(keys, matrix(theirs_ref, 1))
    applied = first * jax.nn.sigmoid(first) * third
    a_mine, a_theirs = own_half(applied, core).astype(BF), own_half(applied, 1 - core).astype(BF)
    rows = out_ref.shape[0] // 2
    copies = []
    for n in range(2):
        lines = slice(n * rows, (n + 1) * rows)
        out_ref[lines, :] = (dot(a_mine[lines], matrix(mine_ref, 2)) + dot(a_theirs[lines], matrix(theirs_ref, 2))).astype(BF)
        at = pl.ds(n * rows, rows)
        copies.append(pltpu.make_async_copy(out_ref.at[at], out_hbm.at[at], sems.at[n]))
        copies[n].start()
    for c in copies:
        c.wait()


def per_device(query_feats, key_feats, value_feats, target, token_rates, row_reach, view_counts, w_first, w_third, w_second):
    _, rows, cols, width = query_feats.shape
    tokens, near = rows * cols, HALO * cols
    n_row, n_plane, n_near, n_far = (lax.axis_size(axes) for axes in (ROW, PLANE, "near", "far"))
    share = HD // 2 // n_plane
    few = share // n_near
    flat = lambda x: x.reshape(tokens, width)
    in_hbm = lambda x: pltpu.with_memory_space_constraint(x, pltpu.HBM)

    block, edge = ((tokens, width), BF), ((2, near, width), BF)
    query, key, value, aim = (in_hbm(flat(x)) for x in (query_feats, key_feats, value_feats, target))
    row_of = lambda dtype: ((1, tokens), dtype)
    to_core, to_chip, query, key, value, aim, rates, reach = call(
        lambda *refs: edges_kernel(cols, *refs),
        [edge] * 2 + [block] * 4 + [row_of(F32), row_of(jnp.int32)],
        [HBM] * 6,
        [pltpu.SemaphoreType.DMA((10,)), pltpu.SMEM(row_reach.shape, jnp.int32)],
    )(query, key, value, aim, in_hbm(token_rates[0]), in_hbm(row_reach))
    next_chip = [p for i in range(1, n_row - 1, 2) for p in ((i, i + 1), (i + 1, i))]
    from_chip = lax.ppermute(to_chip, ROW, next_chip)
    from_core = lax.ppermute(to_core, "row_2", SWAP)

    scaled = call(lambda *refs: scale_kernel(tokens, *refs), block, [SMEM] + [VMEM] * 3)(view_counts, to_core, rates, aim)
    attend = lambda *refs: attend_kernel(rows, cols, n_row * rows, *refs)
    own = call(attend, ((2, tokens, width), BF), [SMEM] + [VMEM] * 7)(
        view_counts, reach, query, key, value, from_core, from_chip, scaled
    )
    other = lax.ppermute(own, "row_2", SWAP)
    ws = w_first[0], w_third[0], w_second[0]
    ahead = lambda *refs: forward_kernel(n_plane, n_near, *refs)
    back, gated, old = call(ahead, [((2, tokens, width), BF), ((tokens, width // 2), BF), ((few, 3 * width), F32)], [VMEM] * 4)(own, *ws)
    grads = lambda *refs: grads_kernel(n_plane, *refs)
    part = call(grads, ((n_plane, 3 * share, width), BF), [VMEM] * 7)(own, back, gated, other, *ws)
    part = exchange(part, PLANE)
    spread = lambda *refs: spread_kernel(n_near, few, *refs)
    part = call(spread, ((n_near, few, 3 * width + 128), BF), [SMEM, VMEM])(view_counts, part)
    part = exchange(part, "near")
    part = call(gather_kernel, ((n_far, few, 3 * width + 128), BF), [VMEM])(part)
    groups = [[(n_near * ((f + 2) % n_far)) + u for f in range(n_far)] for u in range(n_near)]
    part = lax.all_to_all(part, ("far", "near"), 0, 0, tiled=True, axis_index_groups=groups)
    new = call(renew_kernel, ((n_near, few, 3 * width), BF), [VMEM] * 2)(part, old)
    new = exchange(new, "near")
    lines = call(order_kernel, ((n_plane, 3 * share, width), BF), [VMEM])(new)
    mine = exchange(lines, PLANE)
    theirs = lax.ppermute(mine, "row_2", SWAP)
    part = call(half_kernel, ((2, tokens, width), F32), [VMEM] * 2)(own, mine)
    scratch = [pltpu.VMEM((tokens, width), BF), pltpu.SemaphoreType.DMA((2,))]
    out = call(apply_kernel, block, [VMEM] * 4, scratch, HBM)(own, part, mine, theirs)
    return out.reshape(1, rows, cols, width)


def solution(mesh):
    torus = Mesh(
        mesh.devices.reshape(mesh.shape["head"], mesh.shape["view"] // 4, 4, 2, 4, 2),
        ("head", "far", "near", "row_0", "row_1", "row_2"),
    )
    views = ("far", "near")
    feats = P(views, ROW, None, "head")
    heads = P("head", None, None)
    return jax.shard_map(
        per_device,
        mesh=torus,
        in_specs=(feats, feats, feats, feats, P(views, "head", ROW), P(ROW), P(views), heads, heads, heads),
        out_specs=feats,
        check_vma=False,
    )
```

```python
import math

import jax
import jax.numpy as jnp
from jax import lax
from jax.experimental import pallas as pl
from jax.experimental.pallas import tpu as pltpu
from jax.sharding import Mesh
from jax.sharding import PartitionSpec as P

HD = 512
ATT_HD = 128
HALO = 2
PLANE = ("row_0", "row_1")
ROW = ("row_0", "row_1", "row_2")
SWAP = [(0, 1), (1, 0)]
BF = jnp.bfloat16
F32 = jnp.float32
VMEM = pl.BlockSpec(memory_space=pltpu.VMEM)
SMEM = pl.BlockSpec(memory_space=pltpu.SMEM)
HBM = pl.BlockSpec(memory_space=pltpu.HBM)


def dot(a, b, ca=1, cb=0):
    return lax.dot_general(a, b, (((ca,), (cb,)), ((), ())), preferred_element_type=F32)


def led(axes, leader):
    order = list(range(lax.axis_size(axes)))
    order[0], order[leader] = leader, 0
    return order


def exchange(x, axes, order):
    return lax.all_to_all(x, axes, 0, 0, tiled=True, axis_index_groups=[order])


def iota(shape, dim):
    return lax.broadcasted_iota(jnp.int32, shape, dim)


def call(kernel, shapes, specs, scratch=(), out=VMEM):
    many = isinstance(shapes, list)
    outs = [jax.ShapeDtypeStruct(*s) for s in shapes] if many else jax.ShapeDtypeStruct(*shapes)
    return pl.pallas_call(
        kernel,
        out_shape=outs,
        in_specs=specs,
        out_specs=[out] * len(shapes) if many else out,
        scratch_shapes=scratch,
        compiler_params=pltpu.CompilerParams(vmem_limit_bytes=24 << 20),
        cost_estimate=pl.CostEstimate(flops=1 << 20, bytes_accessed=1 << 20, transcendentals=0),
    )


def start_all(pairs, sems):
    copies = [pltpu.make_async_copy(a, b, sems.at[n]) for n, (a, b) in enumerate(pairs)]
    for c in copies:
        c.start()
    return copies


def edges_kernel(
    cols, q_in, k_in, v_in, t_in, rate_in, reach_in, core_ref, chip_ref, q_ref, k_ref, v_ref, t_ref, rate_ref, reach_ref, sems, reach_smem
):
    core = lax.axis_index("row_2")
    near = HALO * cols
    end = k_in.shape[0] - near
    to_core = pl.ds(pl.multiple_of((1 - core) * end, near), near)
    to_chip = pl.ds(pl.multiple_of(core * end, near), near)
    pairs = [(reach_in, reach_smem)]
    for i, ref in enumerate((k_in, v_in)):
        pairs += [(ref.at[to_core], core_ref.at[i]), (ref.at[to_chip], chip_ref.at[i])]
    pairs += [(rate_in, rate_ref), (t_in, t_ref), (q_in, q_ref), (k_in, k_ref), (v_in, v_ref)]
    copies = start_all(pairs, sems)
    copies[0].wait()
    line = iota(reach_ref.shape, 1) // cols
    reach = jnp.zeros(reach_ref.shape, jnp.int32)
    for r in range(reach_smem.shape[0]):
        reach = jnp.where(line == r, reach_smem[r], reach)
    reach_ref[...] = reach
    for c in copies[1:]:
        c.wait()


def scale_kernel(tokens, count_ref, edge_ref, rate_ref, t_ref, out_ref):
    diagonal = iota((tokens, tokens), 0) == iota((tokens, tokens), 1)
    q_tok = lax.axis_index(ROW) * tokens + iota((1, tokens), 1)
    valid = jnp.where(q_tok < count_ref[0], 1.0, 0.0)
    rates = jnp.sum(jnp.where(diagonal, rate_ref[...] * valid, 0.0), 1, keepdims=True)
    out_ref[...] = (rates * t_ref[...].astype(F32)).astype(BF)


def attend_kernel(rows, cols, grid_rows, count_ref, reach_ref, q_ref, k_ref, v_ref, core_ref, chip_ref, scaled_ref, out_ref):
    core = lax.axis_index("row_2")
    base = lax.axis_index(ROW) * rows
    tokens, near = rows * cols, HALO * cols
    span = tokens + 2 * near
    at = iota((span, 1), 0)
    below, above = base + rows, base - HALO
    first_core = jnp.where(core == 0, below, above)
    first_chip = jnp.where(core == 0, above, below)
    start = jnp.where(at < tokens, base, jnp.where(at < tokens + near, first_core, first_chip))
    skip = jnp.where(at < tokens, 0, jnp.where(at < tokens + near, tokens, tokens + near))
    k_tok = start * cols + at - skip
    k_row = start + (at - skip) // cols
    q_at = iota((1, tokens), 1)
    q_row = base + q_at // cols
    q_tok = base * cols + q_at
    valid = (k_tok < count_ref[0]) & (k_row >= 0) & (k_row < grid_rows)
    k_row = jnp.where(valid, k_row, -(1 << 20))
    allowed = (jnp.abs(k_row - q_row) <= reach_ref[...]) | (k_tok == q_tok)
    heads = [slice(at, at + ATT_HD) for at in range(0, q_ref.shape[1], ATT_HD)]
    factor = math.log2(math.e) / math.sqrt(ATT_HD)
    keys = [jnp.concatenate([k_ref[:, h], core_ref[0, :, h], chip_ref[0, :, h]], 0) for h in heads]
    values = [jnp.concatenate([v_ref[:, h], core_ref[1, :, h], chip_ref[1, :, h]], 0) for h in heads]
    scores = [jnp.where(allowed, dot(k, q_ref[:, h], 1, 1), -1e30) for k, h in zip(keys, heads)]
    tops = [jnp.max(s, 0, keepdims=True) for s in scores]
    powers = [jnp.exp2((s - t) * factor) for s, t in zip(scores, tops)]
    sums = [jnp.sum(p, 0, keepdims=True) for p in powers]
    weights = [(p * (1.0 / s)).astype(BF) for p, s in zip(powers, sums)]
    attended = [dot(w, v, 0, 0).astype(BF).astype(F32) for w, v in zip(weights, values)]
    mean = sum(jnp.sum(a * a, -1, keepdims=True) for a in attended) / q_ref.shape[1]
    inverse = lax.rsqrt(mean + 1e-06)
    for a, h in zip(attended, heads):
        out_ref[0, :, h] = (a * inverse).astype(BF)
    out_ref[1] = scaled_ref[...]


def forward(keys, scaled, w1_ref, w3_ref, w2_ref):
    first = dot(keys, w1_ref[...])
    third = dot(keys, w3_ref[...])
    back = dot(scaled, w2_ref[...], 1, 1)
    sig = jax.nn.sigmoid(first)
    silu = first * sig
    back_first = back * third * (sig * (1.0 + first * (1.0 - sig)))
    return back_first.astype(BF), (back * silu).astype(BF), silu * third


def own_half(x, core):
    half = x.shape[1] // 2
    return jnp.where(core == 0, x[:, :half], x[:, half:])


def forward_kernel(n_plane, n_near, own_ref, w1_ref, w3_ref, w2_ref, out_ref, gated_ref, old_ref):
    core = lax.axis_index("row_2")
    half = HD // 2
    share = half // n_plane
    few = share // n_near
    back_first, back_third, gated = forward(own_ref[0], own_ref[1], w1_ref, w3_ref, w2_ref)
    out_ref[0] = back_first
    out_ref[1] = back_third
    gated_ref[...] = own_half(gated, core).astype(BF)
    base = pl.multiple_of(core * half + lax.axis_index(PLANE) * share, share)
    at = lax.axis_index("near") * few
    pick = jnp.where(iota((few, share), 1) == at + iota((few, share), 0), 1.0, 0.0).astype(BF)
    for k, ref in enumerate((w1_ref, w3_ref, w2_ref)):
        old_ref[:, k * HD : (k + 1) * HD] = dot(pick, ref[pl.ds(base, share), :])


def grads_kernel(order, own_ref, mine_ref, mine_gated_ref, other_ref, w1_ref, w3_ref, w2_ref, out_ref):
    core = lax.axis_index("row_2")
    half = HD // 2
    share = half // len(order)
    back_first, back_third, gated = forward(other_ref[0], other_ref[1], w1_ref, w3_ref, w2_ref)
    lanes = pl.ds(pl.multiple_of(core * half, half), half)
    both = lambda a, b: jnp.concatenate([a, b], 0)
    keys = both(own_ref[0, :, lanes], other_ref[0, :, lanes])
    gated = both(mine_gated_ref[...], own_half(gated, core).astype(BF))
    pairs = (
        (keys, both(mine_ref[0], back_first)),
        (keys, both(mine_ref[1], back_third)),
        (gated, both(own_ref[1], other_ref[1])),
    )
    for k, (a, b) in enumerate(pairs):
        g = dot(a, b, 0, 0).astype(BF)
        for n, p in enumerate(order):
            out_ref[n, k * share : (k + 1) * share, :] = g[p * share : (p + 1) * share]


def spread_kernel(order, few, count_ref, x_ref, out_ref):
    total = jnp.sum(x_ref[...].astype(F32), 0)
    share = total.shape[0] // 3
    for k in range(3):
        for n, u in enumerate(order):
            at = k * share + u * few
            out_ref[n, :, k * HD : (k + 1) * HD] = total[at : at + few].astype(BF)
    count = count_ref[0]
    lane = iota((few, 128), 1)
    digits = jnp.where(lane == 0, count % 16, jnp.where(lane == 1, (count // 16) % 16, count // 256))
    digits = digits.astype(F32).astype(BF)
    for n in range(len(order)):
        out_ref[n, :, 3 * HD :] = digits


def gather_kernel(x_ref, out_ref):
    total = jnp.sum(x_ref[...].astype(F32), 0).astype(BF)
    out_ref[...] = jnp.broadcast_to(total[None], out_ref.shape)


def renew_kernel(x_ref, old_ref, out_ref):
    summed = jnp.sum(x_ref[...].astype(F32), 0)
    last = summed[0:1, 3 * HD :]
    total = last[:, 0:1] + 16.0 * last[:, 1:2] + 256.0 * last[:, 2:3]
    for k in range(3):
        lanes = slice(k * HD, (k + 1) * HD)
        old = old_ref[:, lanes]
        raised = old + summed[:, lanes] / total
        rescale = jnp.sqrt(jnp.sum(old * old, -1, keepdims=True) + 1e-06) / jnp.sqrt(
            jnp.sum(raised * raised, -1, keepdims=True) + 1e-06
        )
        new = (raised * rescale).astype(BF)
        for u in range(out_ref.shape[0]):
            out_ref[u, :, lanes] = new


def order_kernel(order, x_ref, out_ref):
    x = x_ref[...].astype(F32)
    lines = jnp.concatenate([x[n, :, k * HD : (k + 1) * HD] for k in range(3) for n in order], 0).astype(BF)
    out_ref[...] = jnp.broadcast_to(lines[None], out_ref.shape)


def matrix(order, ref, k):
    share = ref.shape[1] // 3
    return jnp.concatenate([ref[n, k * share : (k + 1) * share, :] for n in order], 0)


def half_kernel(order, own_ref, mine_ref, out_ref):
    half = HD // 2
    keys = own_ref[0, :, pl.ds(pl.multiple_of(lax.axis_index("row_2") * half, half), half)]
    out_ref[0] = dot(keys, matrix(order, mine_ref, 0))
    out_ref[1] = dot(keys, matrix(order, mine_ref, 1))


def apply_kernel(order, own_ref, part_ref, mine_ref, theirs_ref, out_hbm, out_ref, sems):
    core = lax.axis_index("row_2")
    half = HD // 2
    keys = own_ref[0, :, pl.ds(pl.multiple_of((1 - core) * half, half), half)]
    first = part_ref[0] + dot(keys, matrix(order, theirs_ref, 0))
    third = part_ref[1] + dot(keys, matrix(order, theirs_ref, 1))
    applied = first * jax.nn.sigmoid(first) * third
    a_mine, a_theirs = own_half(applied, core).astype(BF), own_half(applied, 1 - core).astype(BF)
    rows = out_ref.shape[0] // 2
    copies = []
    for n in range(2):
        lines = slice(n * rows, (n + 1) * rows)
        out_ref[lines, :] = (dot(a_mine[lines], matrix(order, mine_ref, 2)) + dot(a_theirs[lines], matrix(order, theirs_ref, 2))).astype(BF)
        at = pl.ds(n * rows, rows)
        copies.append(pltpu.make_async_copy(out_ref.at[at], out_hbm.at[at], sems.at[n]))
        copies[n].start()
    for c in copies:
        c.wait()


def per_device(query_feats, key_feats, value_feats, target, token_rates, row_reach, view_counts, w_first, w_third, w_second):
    _, rows, cols, width = query_feats.shape
    tokens, near = rows * cols, HALO * cols
    n_row, n_plane, n_near, n_far = (lax.axis_size(axes) for axes in (ROW, PLANE, "near", "far"))
    share = HD // 2 // n_plane
    few = share // n_near
    flat = lambda x: x.reshape(tokens, width)
    in_hbm = lambda x: pltpu.with_memory_space_constraint(x, pltpu.HBM)

    block, edge = ((tokens, width), BF), ((2, near, width), BF)
    query, key, value, aim = (in_hbm(flat(x)) for x in (query_feats, key_feats, value_feats, target))
    row_of = lambda dtype: ((1, tokens), dtype)
    to_core, to_chip, query, key, value, aim, rates, reach = call(
        lambda *refs: edges_kernel(cols, *refs),
        [edge] * 2 + [block] * 4 + [row_of(F32), row_of(jnp.int32)],
        [HBM] * 6,
        [pltpu.SemaphoreType.DMA((10,)), pltpu.SMEM(row_reach.shape, jnp.int32)],
    )(query, key, value, aim, in_hbm(token_rates[0]), in_hbm(row_reach))
    next_chip = [p for i in range(1, n_row - 1, 2) for p in ((i, i + 1), (i + 1, i))]
    from_chip = lax.ppermute(to_chip, ROW, next_chip)
    from_core = lax.ppermute(to_core, "row_2", SWAP)

    scaled = call(lambda *refs: scale_kernel(tokens, *refs), block, [SMEM] + [VMEM] * 3)(view_counts, to_core, rates, aim)
    attend = lambda *refs: attend_kernel(rows, cols, n_row * rows, *refs)
    own = call(attend, ((2, tokens, width), BF), [SMEM] + [VMEM] * 7)(
        view_counts, reach, query, key, value, from_core, from_chip, scaled
    )
    other = lax.ppermute(own, "row_2", SWAP)
    ws = w_first[0], w_third[0], w_second[0]
    ahead = lambda *refs: forward_kernel(n_plane, n_near, *refs)
    back, gated, old = call(ahead, [((2, tokens, width), BF), ((tokens, width // 2), BF), ((few, 3 * width), F32)], [VMEM] * 4)(own, *ws)
    planes, nears = led(PLANE, n_plane - 2), led("near", n_near - 2)
    grads = lambda *refs: grads_kernel(planes, *refs)
    part = call(grads, ((n_plane, 3 * share, width), BF), [VMEM] * 7)(own, back, gated, other, *ws)
    part = exchange(part, PLANE, planes)
    spread = lambda *refs: spread_kernel(nears, few, *refs)
    part = call(spread, ((n_near, few, 3 * width + 128), BF), [SMEM, VMEM])(view_counts, part)
    part = exchange(part, "near", nears)
    part = call(gather_kernel, ((n_far, few, 3 * width + 128), BF), [VMEM])(part)
    part = exchange(part, "far", led("far", n_far // 2))
    new = call(renew_kernel, ((n_near, few, 3 * width), BF), [VMEM] * 2)(part, old)
    new = exchange(new, "near", nears)
    lines = call(lambda *refs: order_kernel(nears, *refs), ((n_plane, 3 * share, width), BF), [VMEM])(new)
    mine = exchange(lines, PLANE, planes)
    theirs = lax.ppermute(mine, "row_2", SWAP)
    part = call(lambda *refs: half_kernel(planes, *refs), ((2, tokens, width), F32), [VMEM] * 2)(own, mine)
    scratch = [pltpu.VMEM((tokens, width), BF), pltpu.SemaphoreType.DMA((2,))]
    out = call(lambda *refs: apply_kernel(planes, *refs), block, [VMEM] * 4, scratch, HBM)(own, part, mine, theirs)
    return out.reshape(1, rows, cols, width)


def solution(mesh):
    torus = Mesh(
        mesh.devices.reshape(mesh.shape["head"], mesh.shape["view"] // 4, 4, 2, 4, 2),
        ("head", "far", "near", "row_0", "row_1", "row_2"),
    )
    views = ("far", "near")
    feats = P(views, ROW, None, "head")
    heads = P("head", None, None)
    return jax.shard_map(
        per_device,
        mesh=torus,
        in_specs=(feats, feats, feats, feats, P(views, "head", ROW), P(ROW), P(views), heads, heads, heads),
        out_specs=feats,
        check_vma=False,
    )
```

```python
import math

import jax
import jax.numpy as jnp
from jax import lax
from jax.experimental import pallas as pl
from jax.experimental.pallas import tpu as pltpu
from jax.sharding import Mesh
from jax.sharding import PartitionSpec as P

HD = 512
ATT_HD = 128
HALO = 2
PLANE = ("row_0", "row_1")
ROW = ("row_0", "row_1", "row_2")
SWAP = [(0, 1), (1, 0)]
BF = jnp.bfloat16
F32 = jnp.float32
VMEM = pl.BlockSpec(memory_space=pltpu.VMEM)
SMEM = pl.BlockSpec(memory_space=pltpu.SMEM)
HBM = pl.BlockSpec(memory_space=pltpu.HBM)


def dot(a, b, ca=1, cb=0):
    return lax.dot_general(a, b, (((ca,), (cb,)), ((), ())), preferred_element_type=F32)


def led(axes, leader):
    return [leader ^ i for i in range(lax.axis_size(axes))]


def exchange(x, axes, order):
    return lax.all_to_all(x, axes, 0, 0, tiled=True, axis_index_groups=[order])


def iota(shape, dim):
    return lax.broadcasted_iota(jnp.int32, shape, dim)


def call(kernel, shapes, specs, scratch=(), out=VMEM):
    many = isinstance(shapes, list)
    outs = [jax.ShapeDtypeStruct(*s) for s in shapes] if many else jax.ShapeDtypeStruct(*shapes)
    return pl.pallas_call(
        kernel,
        out_shape=outs,
        in_specs=specs,
        out_specs=[out] * len(shapes) if many else out,
        scratch_shapes=scratch,
        compiler_params=pltpu.CompilerParams(vmem_limit_bytes=24 << 20),
        cost_estimate=pl.CostEstimate(flops=1 << 20, bytes_accessed=1 << 20, transcendentals=0),
    )


def start_all(pairs, sems):
    copies = [pltpu.make_async_copy(a, b, sems.at[n]) for n, (a, b) in enumerate(pairs)]
    for c in copies:
        c.start()
    return copies


def edges_kernel(cols, k_in, v_in, rate_in, reach_in, core_ref, chip_ref, rate_ref, reach_ref, sems, reach_smem):
    core = lax.axis_index("row_2")
    near = HALO * cols
    end = k_in.shape[0] - near
    to_core = pl.ds(pl.multiple_of((1 - core) * end, near), near)
    to_chip = pl.ds(pl.multiple_of(core * end, near), near)
    pairs = [(reach_in, reach_smem), (rate_in, rate_ref)]
    for i, ref in enumerate((k_in, v_in)):
        pairs += [(ref.at[to_core], core_ref.at[i]), (ref.at[to_chip], chip_ref.at[i])]
    copies = start_all(pairs, sems)
    copies[0].wait()
    line = iota(reach_ref.shape, 1) // cols
    reach = jnp.zeros(reach_ref.shape, jnp.int32)
    for r in range(reach_smem.shape[0]):
        reach = jnp.where(line == r, reach_smem[r], reach)
    reach_ref[...] = reach
    for c in copies[1:]:
        c.wait()


def load_kernel(count_ref, edge_ref, rate_ref, t_in, q_in, k_in, v_in, scaled_ref, q_ref, k_ref, v_ref, sems, t_ref):
    copies = start_all([(t_in, t_ref), (q_in, q_ref), (k_in, k_ref), (v_in, v_ref)], sems)
    tokens = t_ref.shape[0]
    diagonal = iota((tokens, tokens), 0) == iota((tokens, tokens), 1)
    q_tok = lax.axis_index(ROW) * tokens + iota((1, tokens), 1)
    valid = jnp.where(q_tok < count_ref[0], 1.0, 0.0)
    rates = jnp.sum(jnp.where(diagonal, rate_ref[...] * valid, 0.0), 1, keepdims=True)
    copies[0].wait()
    scaled_ref[...] = (rates * t_ref[...].astype(F32)).astype(BF)
    for c in copies[1:]:
        c.wait()


def attend_kernel(rows, cols, grid_rows, count_ref, reach_ref, q_ref, k_ref, v_ref, core_ref, chip_ref, scaled_ref, out_ref):
    core = lax.axis_index("row_2")
    base = lax.axis_index(ROW) * rows
    tokens, near = rows * cols, HALO * cols
    span = tokens + 2 * near
    at = iota((span, 1), 0)
    below, above = base + rows, base - HALO
    first_core = jnp.where(core == 0, below, above)
    first_chip = jnp.where(core == 0, above, below)
    start = jnp.where(at < tokens, base, jnp.where(at < tokens + near, first_core, first_chip))
    skip = jnp.where(at < tokens, 0, jnp.where(at < tokens + near, tokens, tokens + near))
    k_tok = start * cols + at - skip
    k_row = start + (at - skip) // cols
    q_at = iota((1, tokens), 1)
    q_row = base + q_at // cols
    q_tok = base * cols + q_at
    valid = (k_tok < count_ref[0]) & (k_row >= 0) & (k_row < grid_rows)
    k_row = jnp.where(valid, k_row, -(1 << 20))
    allowed = (jnp.abs(k_row - q_row) <= reach_ref[...]) | (k_tok == q_tok)
    heads = [slice(at, at + ATT_HD) for at in range(0, q_ref.shape[1], ATT_HD)]
    factor = math.log2(math.e) / math.sqrt(ATT_HD)
    keys = [jnp.concatenate([k_ref[:, h], core_ref[0, :, h], chip_ref[0, :, h]], 0) for h in heads]
    values = [jnp.concatenate([v_ref[:, h], core_ref[1, :, h], chip_ref[1, :, h]], 0) for h in heads]
    scores = [jnp.where(allowed, dot(k, q_ref[:, h], 1, 1), -1e30) for k, h in zip(keys, heads)]
    tops = [jnp.max(s, 0, keepdims=True) for s in scores]
    powers = [jnp.exp2((s - t) * factor) for s, t in zip(scores, tops)]
    sums = [jnp.sum(p, 0, keepdims=True) for p in powers]
    weights = [(p * (1.0 / s)).astype(BF) for p, s in zip(powers, sums)]
    attended = [dot(w, v, 0, 0).astype(BF).astype(F32) for w, v in zip(weights, values)]
    mean = sum(jnp.sum(a * a, -1, keepdims=True) for a in attended) / q_ref.shape[1]
    inverse = lax.rsqrt(mean + 1e-06)
    for a, h in zip(attended, heads):
        out_ref[0, :, h] = (a * inverse).astype(BF)
    out_ref[1] = scaled_ref[...]


def forward(keys, scaled, w1_ref, w3_ref, w2_ref):
    first = dot(keys, w1_ref[...])
    third = dot(keys, w3_ref[...])
    back = dot(scaled, w2_ref[...], 1, 1)
    sig = jax.nn.sigmoid(first)
    silu = first * sig
    back_first = back * third * (sig * (1.0 + first * (1.0 - sig)))
    return back_first.astype(BF), (back * silu).astype(BF), silu * third


def own_half(x, core):
    half = x.shape[1] // 2
    return jnp.where(core == 0, x[:, :half], x[:, half:])


def forward_kernel(n_plane, n_near, own_ref, w1_ref, w3_ref, w2_ref, out_ref, gated_ref, old_ref):
    core = lax.axis_index("row_2")
    half = HD // 2
    share = half // n_plane
    few = share // n_near
    back_first, back_third, gated = forward(own_ref[0], own_ref[1], w1_ref, w3_ref, w2_ref)
    out_ref[0] = back_first
    out_ref[1] = back_third
    gated_ref[...] = own_half(gated, core).astype(BF)
    base = pl.multiple_of(core * half + lax.axis_index(PLANE) * share, share)
    at = lax.axis_index("near") * few
    pick = jnp.where(iota((few, share), 1) == at + iota((few, share), 0), 1.0, 0.0).astype(BF)
    for k, ref in enumerate((w1_ref, w3_ref, w2_ref)):
        old_ref[:, k * HD : (k + 1) * HD] = dot(pick, ref[pl.ds(base, share), :])


def grads_kernel(order, own_ref, mine_ref, mine_gated_ref, other_ref, w1_ref, w3_ref, w2_ref, out_ref):
    core = lax.axis_index("row_2")
    half = HD // 2
    share = half // len(order)
    back_first, back_third, gated = forward(other_ref[0], other_ref[1], w1_ref, w3_ref, w2_ref)
    lanes = pl.ds(pl.multiple_of(core * half, half), half)
    both = lambda a, b: jnp.concatenate([a, b], 0)
    keys = both(own_ref[0, :, lanes], other_ref[0, :, lanes])
    gated = both(mine_gated_ref[...], own_half(gated, core).astype(BF))
    pairs = (
        (keys, both(mine_ref[0], back_first)),
        (keys, both(mine_ref[1], back_third)),
        (gated, both(own_ref[1], other_ref[1])),
    )
    for k, (a, b) in enumerate(pairs):
        g = dot(a, b, 0, 0).astype(BF)
        for n, p in enumerate(order):
            out_ref[n, k * share : (k + 1) * share, :] = g[p * share : (p + 1) * share]


def spread_kernel(order, few, count_ref, x_ref, out_ref):
    total = jnp.sum(x_ref[...].astype(F32), 0)
    share = total.shape[0] // 3
    for k in range(3):
        for n, u in enumerate(order):
            at = k * share + u * few
            out_ref[n, :, k * HD : (k + 1) * HD] = total[at : at + few].astype(BF)
    count = count_ref[0]
    lane = iota((few, 128), 1)
    digits = jnp.where(lane == 0, count % 16, jnp.where(lane == 1, (count // 16) % 16, count // 256))
    digits = digits.astype(F32).astype(BF)
    for n in range(len(order)):
        out_ref[n, :, 3 * HD :] = digits


def gather_kernel(x_ref, out_ref):
    total = jnp.sum(x_ref[...].astype(F32), 0).astype(BF)
    out_ref[...] = jnp.broadcast_to(total[None], out_ref.shape)


def renew_kernel(x_ref, old_ref, out_ref):
    summed = jnp.sum(x_ref[...].astype(F32), 0)
    last = summed[0:1, 3 * HD :]
    total = last[:, 0:1] + 16.0 * last[:, 1:2] + 256.0 * last[:, 2:3]
    for k in range(3):
        lanes = slice(k * HD, (k + 1) * HD)
        old = old_ref[:, lanes]
        raised = old + summed[:, lanes] / total
        rescale = jnp.sqrt(jnp.sum(old * old, -1, keepdims=True) + 1e-06) / jnp.sqrt(
            jnp.sum(raised * raised, -1, keepdims=True) + 1e-06
        )
        new = (raised * rescale).astype(BF)
        for u in range(out_ref.shape[0]):
            out_ref[u, :, lanes] = new


def order_kernel(order, x_ref, out_ref):
    x = x_ref[...].astype(F32)
    lines = jnp.concatenate([x[n, :, k * HD : (k + 1) * HD] for k in range(3) for n in order], 0).astype(BF)
    out_ref[...] = jnp.broadcast_to(lines[None], out_ref.shape)


def matrix(order, ref, k):
    share = ref.shape[1] // 3
    return jnp.concatenate([ref[n, k * share : (k + 1) * share, :] for n in order], 0)


def half_kernel(order, own_ref, mine_ref, out_ref):
    half = HD // 2
    keys = own_ref[0, :, pl.ds(pl.multiple_of(lax.axis_index("row_2") * half, half), half)]
    out_ref[0] = dot(keys, matrix(order, mine_ref, 0))
    out_ref[1] = dot(keys, matrix(order, mine_ref, 1))


def apply_kernel(order, own_ref, part_ref, mine_ref, theirs_ref, out_hbm, out_ref, sems):
    core = lax.axis_index("row_2")
    half = HD // 2
    keys = own_ref[0, :, pl.ds(pl.multiple_of((1 - core) * half, half), half)]
    first = part_ref[0] + dot(keys, matrix(order, theirs_ref, 0))
    third = part_ref[1] + dot(keys, matrix(order, theirs_ref, 1))
    applied = first * jax.nn.sigmoid(first) * third
    a_mine, a_theirs = own_half(applied, core).astype(BF), own_half(applied, 1 - core).astype(BF)
    rows = out_ref.shape[0] // 2
    copies = []
    for n in range(2):
        lines = slice(n * rows, (n + 1) * rows)
        out_ref[lines, :] = (dot(a_mine[lines], matrix(order, mine_ref, 2)) + dot(a_theirs[lines], matrix(order, theirs_ref, 2))).astype(BF)
        at = pl.ds(n * rows, rows)
        copies.append(pltpu.make_async_copy(out_ref.at[at], out_hbm.at[at], sems.at[n]))
        copies[n].start()
    for c in copies:
        c.wait()


def per_device(query_feats, key_feats, value_feats, target, token_rates, row_reach, view_counts, w_first, w_third, w_second):
    _, rows, cols, width = query_feats.shape
    tokens, near = rows * cols, HALO * cols
    n_row, n_plane, n_near, n_far = (lax.axis_size(axes) for axes in (ROW, PLANE, "near", "far"))
    share = HD // 2 // n_plane
    few = share // n_near
    flat = lambda x: x.reshape(tokens, width)
    in_hbm = lambda x: pltpu.with_memory_space_constraint(x, pltpu.HBM)

    block, edge = ((tokens, width), BF), ((2, near, width), BF)
    query, key, value, aim = (in_hbm(flat(x)) for x in (query_feats, key_feats, value_feats, target))
    row_of = lambda dtype: ((1, tokens), dtype)
    to_core, to_chip, rates, reach = call(
        lambda *refs: edges_kernel(cols, *refs),
        [edge] * 2 + [row_of(F32), row_of(jnp.int32)],
        [HBM] * 4,
        [pltpu.SemaphoreType.DMA((6,)), pltpu.SMEM(row_reach.shape, jnp.int32)],
    )(key, value, *(in_hbm(x) for x in (token_rates[0], row_reach)))
    next_chip = [p for i in range(1, n_row - 1, 2) for p in ((i, i + 1), (i + 1, i))]
    from_chip = lax.ppermute(to_chip, ROW, next_chip)
    from_core = lax.ppermute(to_core, "row_2", SWAP)

    scaled, query, key, value = call(
        load_kernel, [block] * 4, [SMEM] + [VMEM] * 2 + [HBM] * 4, [pltpu.SemaphoreType.DMA((4,)), pltpu.VMEM((tokens, width), BF)]
    )(view_counts, to_core, rates, aim, query, key, value)
    attend = lambda *refs: attend_kernel(rows, cols, n_row * rows, *refs)
    own = call(attend, ((2, tokens, width), BF), [SMEM] + [VMEM] * 7)(view_counts, reach, query, key, value, from_core, from_chip, scaled)
    other = lax.ppermute(own, "row_2", SWAP)
    ws = w_first[0], w_third[0], w_second[0]
    ahead = lambda *refs: forward_kernel(n_plane, n_near, *refs)
    back, gated, old = call(ahead, [((2, tokens, width), BF), ((tokens, width // 2), BF), ((few, 3 * width), F32)], [VMEM] * 4)(own, *ws)
    planes, nears = led(PLANE, n_plane - 1), led("near", n_near - 2)
    planes_late, nears_late = led(PLANE, n_plane - 2), led("near", n_near - 1)
    grads = lambda *refs: grads_kernel(planes, *refs)
    part = call(grads, ((n_plane, 3 * share, width), BF), [VMEM] * 7)(own, back, gated, other, *ws)
    part = exchange(part, PLANE, planes)
    spread = lambda *refs: spread_kernel(nears, few, *refs)
    part = call(spread, ((n_near, few, 3 * width + 128), BF), [SMEM, VMEM])(view_counts, part)
    part = exchange(part, "near", nears)
    part = call(gather_kernel, ((n_far, few, 3 * width + 128), BF), [VMEM])(part)
    part = exchange(part, "far", led("far", n_far // 2))
    new = call(renew_kernel, ((n_near, few, 3 * width), BF), [VMEM] * 2)(part, old)
    new = exchange(new, "near", nears_late)
    lines = call(lambda *refs: order_kernel(nears_late, *refs), ((n_plane, 3 * share, width), BF), [VMEM])(new)
    mine = exchange(lines, PLANE, planes_late)
    theirs = lax.ppermute(mine, "row_2", SWAP)
    part = call(lambda *refs: half_kernel(planes_late, *refs), ((2, tokens, width), F32), [VMEM] * 2)(own, mine)
    scratch = [pltpu.VMEM((tokens, width), BF), pltpu.SemaphoreType.DMA((2,))]
    out = call(lambda *refs: apply_kernel(planes_late, *refs), block, [VMEM] * 4, scratch, HBM)(own, part, mine, theirs)
    return out.reshape(1, rows, cols, width)


def solution(mesh):
    torus = Mesh(
        mesh.devices.reshape(mesh.shape["head"], mesh.shape["view"] // 4, 4, 2, 4, 2),
        ("head", "far", "near", "row_0", "row_1", "row_2"),
    )
    views = ("far", "near")
    feats = P(views, ROW, None, "head")
    heads = P("head", None, None)
    return jax.shard_map(
        per_device,
        mesh=torus,
        in_specs=(feats, feats, feats, feats, P(views, "head", ROW), P(ROW), P(views), heads, heads, heads),
        out_specs=feats,
        check_vma=False,
    )
```

```python
import math

import jax
import jax.numpy as jnp
from jax import lax
from jax.experimental import pallas as pl
from jax.experimental.pallas import tpu as pltpu
from jax.sharding import Mesh
from jax.sharding import PartitionSpec as P

HD = 512
ATT_HD = 128
HALO = 2
PLANE = ("row_0", "row_1")
ROW = ("row_0", "row_1", "row_2")
SWAP = [(0, 1), (1, 0)]
BF = jnp.bfloat16
F32 = jnp.float32
VMEM = pl.BlockSpec(memory_space=pltpu.VMEM)
HBM = pl.BlockSpec(memory_space=pltpu.HBM)


def dot(a, b, ca=1, cb=0):
    return lax.dot_general(a, b, (((ca,), (cb,)), ((), ())), preferred_element_type=F32)


def led(axes, leader):
    return [leader ^ i for i in range(lax.axis_size(axes))]


def exchange(x, axes, order):
    return lax.all_to_all(x, axes, 0, 0, tiled=True, axis_index_groups=[order])


def iota(shape, dim):
    return lax.broadcasted_iota(jnp.int32, shape, dim)


def call(kernel, shapes, specs, scratch=(), out=VMEM):
    many = isinstance(shapes, list)
    outs = [jax.ShapeDtypeStruct(*s) for s in shapes] if many else jax.ShapeDtypeStruct(*shapes)
    return pl.pallas_call(
        kernel,
        out_shape=outs,
        in_specs=specs,
        out_specs=[out] * len(shapes) if many else out,
        scratch_shapes=scratch,
        compiler_params=pltpu.CompilerParams(vmem_limit_bytes=24 << 20),
        cost_estimate=pl.CostEstimate(flops=1 << 20, bytes_accessed=1 << 20, transcendentals=0),
    )


def start_all(pairs, sems):
    copies = [pltpu.make_async_copy(a, b, sems.at[n]) for n, (a, b) in enumerate(pairs)]
    for c in copies:
        c.start()
    return copies


def edges_kernel(cols, k_in, v_in, rate_in, reach_in, core_ref, chip_ref, rate_ref, reach_ref, sems, reach_smem):
    core = lax.axis_index("row_2")
    near = HALO * cols
    end = k_in.shape[0] - near
    to_core = pl.ds(pl.multiple_of((1 - core) * end, near), near)
    to_chip = pl.ds(pl.multiple_of(core * end, near), near)
    pairs = [(reach_in, reach_smem), (rate_in, rate_ref)]
    for i, ref in enumerate((k_in, v_in)):
        pairs += [(ref.at[to_core], core_ref.at[i]), (ref.at[to_chip], chip_ref.at[i])]
    copies = start_all(pairs, sems)
    copies[0].wait()
    line = iota(reach_ref.shape, 1) // cols
    reach = jnp.zeros(reach_ref.shape, jnp.int32)
    for r in range(reach_smem.shape[0]):
        reach = jnp.where(line == r, reach_smem[r], reach)
    reach_ref[...] = reach
    for c in copies[1:]:
        c.wait()


def load_kernel(count_ref, edge_ref, rate_ref, t_in, q_in, k_in, v_in, scaled_ref, q_ref, k_ref, v_ref, sems, t_ref):
    copies = start_all([(t_in, t_ref), (q_in, q_ref), (k_in, k_ref), (v_in, v_ref)], sems)
    tokens = t_ref.shape[0]
    diagonal = iota((tokens, tokens), 0) == iota((tokens, tokens), 1)
    q_tok = lax.axis_index(ROW) * tokens + iota((1, tokens), 1)
    valid = jnp.where(q_tok < count_ref[...], 1.0, 0.0)
    rates = jnp.sum(jnp.where(diagonal, rate_ref[...] * valid, 0.0), 1, keepdims=True)
    copies[0].wait()
    scaled_ref[...] = (rates * t_ref[...].astype(F32)).astype(BF)
    for c in copies[1:]:
        c.wait()


def attend_kernel(rows, cols, grid_rows, count_ref, reach_ref, q_ref, k_ref, v_ref, core_ref, chip_ref, scaled_ref, out_ref):
    core = lax.axis_index("row_2")
    base = lax.axis_index(ROW) * rows
    tokens, near = rows * cols, HALO * cols
    span = tokens + 2 * near
    at = iota((span, 1), 0)
    below, above = base + rows, base - HALO
    first_core = jnp.where(core == 0, below, above)
    first_chip = jnp.where(core == 0, above, below)
    start = jnp.where(at < tokens, base, jnp.where(at < tokens + near, first_core, first_chip))
    skip = jnp.where(at < tokens, 0, jnp.where(at < tokens + near, tokens, tokens + near))
    k_tok = start * cols + at - skip
    k_row = start + (at - skip) // cols
    q_at = iota((1, tokens), 1)
    q_row = base + q_at // cols
    q_tok = base * cols + q_at
    valid = (k_tok < count_ref[...]) & (k_row >= 0) & (k_row < grid_rows)
    k_row = jnp.where(valid, k_row, -(1 << 20))
    allowed = (jnp.abs(k_row - q_row) <= reach_ref[...]) | (k_tok == q_tok)
    heads = [slice(at, at + ATT_HD) for at in range(0, q_ref.shape[1], ATT_HD)]
    factor = math.log2(math.e) / math.sqrt(ATT_HD)
    keys = [jnp.concatenate([k_ref[:, h], core_ref[0, :, h], chip_ref[0, :, h]], 0) for h in heads]
    values = [jnp.concatenate([v_ref[:, h], core_ref[1, :, h], chip_ref[1, :, h]], 0) for h in heads]
    scores = [jnp.where(allowed, dot(k, q_ref[:, h], 1, 1), -1e30) for k, h in zip(keys, heads)]
    tops = [jnp.max(s, 0, keepdims=True) for s in scores]
    powers = [jnp.exp2((s - t) * factor) for s, t in zip(scores, tops)]
    sums = [jnp.sum(p, 0, keepdims=True) for p in powers]
    weights = [(p * (1.0 / s)).astype(BF) for p, s in zip(powers, sums)]
    attended = [dot(w, v, 0, 0).astype(BF).astype(F32) for w, v in zip(weights, values)]
    mean = sum(jnp.sum(a * a, -1, keepdims=True) for a in attended) / q_ref.shape[1]
    inverse = lax.rsqrt(mean + 1e-06)
    for a, h in zip(attended, heads):
        out_ref[0, :, h] = (a * inverse).astype(BF)
    out_ref[1] = scaled_ref[...]


def forward(keys, scaled, w1_ref, w3_ref, w2_ref):
    first = dot(keys, w1_ref[...])
    third = dot(keys, w3_ref[...])
    back = dot(scaled, w2_ref[...], 1, 1)
    sig = jax.nn.sigmoid(first)
    silu = first * sig
    back_first = back * third * (sig * (1.0 + first * (1.0 - sig)))
    return back_first.astype(BF), (back * silu).astype(BF), silu * third


def own_half(x, core):
    half = x.shape[1] // 2
    return jnp.where(core == 0, x[:, :half], x[:, half:])


def forward_kernel(n_plane, n_near, own_ref, w1_ref, w3_ref, w2_ref, out_ref, gated_ref, old_ref):
    core = lax.axis_index("row_2")
    half = HD // 2
    share = half // n_plane
    few = share // n_near
    back_first, back_third, gated = forward(own_ref[0], own_ref[1], w1_ref, w3_ref, w2_ref)
    out_ref[0] = back_first
    out_ref[1] = back_third
    gated_ref[...] = own_half(gated, core).astype(BF)
    base = pl.multiple_of(core * half + lax.axis_index(PLANE) * share, share)
    at = lax.axis_index("near") * few
    pick = jnp.where(iota((few, share), 1) == at + iota((few, share), 0), 1.0, 0.0).astype(BF)
    for k, ref in enumerate((w1_ref, w3_ref, w2_ref)):
        old_ref[:, k * HD : (k + 1) * HD] = dot(pick, ref[pl.ds(base, share), :])


def grads_kernel(order, own_ref, mine_ref, mine_gated_ref, other_ref, w1_ref, w3_ref, w2_ref, out_ref):
    core = lax.axis_index("row_2")
    half = HD // 2
    share = half // len(order)
    back_first, back_third, gated = forward(other_ref[0], other_ref[1], w1_ref, w3_ref, w2_ref)
    lanes = pl.ds(pl.multiple_of(core * half, half), half)
    both = lambda a, b: jnp.concatenate([a, b], 0)
    keys = both(own_ref[0, :, lanes], other_ref[0, :, lanes])
    gated = both(mine_gated_ref[...], own_half(gated, core).astype(BF))
    pairs = (
        (keys, both(mine_ref[0], back_first)),
        (keys, both(mine_ref[1], back_third)),
        (gated, both(own_ref[1], other_ref[1])),
    )
    for k, (a, b) in enumerate(pairs):
        g = dot(a, b, 0, 0).astype(BF)
        for n, p in enumerate(order):
            out_ref[n, k * share : (k + 1) * share, :] = g[p * share : (p + 1) * share]


def spread_kernel(order, few, count_ref, x_ref, out_ref):
    total = jnp.sum(x_ref[...].astype(F32), 0)
    share = total.shape[0] // 3
    for k in range(3):
        for n, u in enumerate(order):
            at = k * share + u * few
            out_ref[n, :, k * HD : (k + 1) * HD] = total[at : at + few].astype(BF)
    lane = iota((few, 128), 1)
    count = jnp.broadcast_to(count_ref[...], lane.shape)
    digits = jnp.where(lane == 0, count % 16, jnp.where(lane == 1, (count // 16) % 16, count // 256))
    digits = digits.astype(F32).astype(BF)
    for n in range(len(order)):
        out_ref[n, :, 3 * HD :] = digits


def gather_kernel(x_ref, out_ref):
    total = jnp.sum(x_ref[...].astype(F32), 0).astype(BF)
    out_ref[...] = jnp.broadcast_to(total[None], out_ref.shape)


def renew_kernel(x_ref, old_ref, out_ref):
    summed = jnp.sum(x_ref[...].astype(F32), 0)
    last = summed[0:1, 3 * HD :]
    total = last[:, 0:1] + 16.0 * last[:, 1:2] + 256.0 * last[:, 2:3]
    for k in range(3):
        lanes = slice(k * HD, (k + 1) * HD)
        old = old_ref[:, lanes]
        raised = old + summed[:, lanes] / total
        rescale = jnp.sqrt(jnp.sum(old * old, -1, keepdims=True) + 1e-06) / jnp.sqrt(
            jnp.sum(raised * raised, -1, keepdims=True) + 1e-06
        )
        new = (raised * rescale).astype(BF)
        for u in range(out_ref.shape[0]):
            out_ref[u, :, lanes] = new


def order_kernel(order, x_ref, out_ref):
    x = x_ref[...].astype(F32)
    lines = jnp.concatenate([x[n, :, k * HD : (k + 1) * HD] for k in range(3) for n in order], 0).astype(BF)
    out_ref[...] = jnp.broadcast_to(lines[None], out_ref.shape)


def matrix(order, ref, k):
    share = ref.shape[1] // 3
    return jnp.concatenate([ref[n, k * share : (k + 1) * share, :] for n in order], 0)


def half_kernel(order, own_ref, mine_ref, out_ref):
    half = HD // 2
    keys = own_ref[0, :, pl.ds(pl.multiple_of(lax.axis_index("row_2") * half, half), half)]
    out_ref[0] = dot(keys, matrix(order, mine_ref, 0))
    out_ref[1] = dot(keys, matrix(order, mine_ref, 1))


def apply_kernel(order, own_ref, part_ref, mine_ref, theirs_ref, out_hbm, out_ref, sems):
    core = lax.axis_index("row_2")
    half = HD // 2
    keys = own_ref[0, :, pl.ds(pl.multiple_of((1 - core) * half, half), half)]
    first = part_ref[0] + dot(keys, matrix(order, theirs_ref, 0))
    third = part_ref[1] + dot(keys, matrix(order, theirs_ref, 1))
    applied = first * jax.nn.sigmoid(first) * third
    a_mine, a_theirs = own_half(applied, core).astype(BF), own_half(applied, 1 - core).astype(BF)
    rows = out_ref.shape[0] // 2
    copies = []
    for n in range(2):
        lines = slice(n * rows, (n + 1) * rows)
        out_ref[lines, :] = (dot(a_mine[lines], matrix(order, mine_ref, 2)) + dot(a_theirs[lines], matrix(order, theirs_ref, 2))).astype(BF)
        at = pl.ds(n * rows, rows)
        copies.append(pltpu.make_async_copy(out_ref.at[at], out_hbm.at[at], sems.at[n]))
        copies[n].start()
    for c in copies:
        c.wait()


def per_device(query_feats, key_feats, value_feats, target, token_rates, row_reach, view_counts, w_first, w_third, w_second):
    _, rows, cols, width = query_feats.shape
    tokens, near = rows * cols, HALO * cols
    n_row, n_plane, n_near, n_far = (lax.axis_size(axes) for axes in (ROW, PLANE, "near", "far"))
    share = HD // 2 // n_plane
    few = share // n_near
    flat = lambda x: x.reshape(tokens, width)
    in_hbm = lambda x: pltpu.with_memory_space_constraint(x, pltpu.HBM)

    block, edge = ((tokens, width), BF), ((2, near, width), BF)
    query, key, value, aim = (in_hbm(flat(x)) for x in (query_feats, key_feats, value_feats, target))
    count = view_counts.reshape(1, 1)
    row_of = lambda dtype: ((1, tokens), dtype)
    to_core, to_chip, rates, reach = call(
        lambda *refs: edges_kernel(cols, *refs),
        [edge] * 2 + [row_of(F32), row_of(jnp.int32)],
        [HBM] * 4,
        [pltpu.SemaphoreType.DMA((6,)), pltpu.SMEM(row_reach.shape, jnp.int32)],
    )(key, value, *(in_hbm(x) for x in (token_rates[0], row_reach)))
    next_chip = [p for i in range(1, n_row - 1, 2) for p in ((i, i + 1), (i + 1, i))]
    from_chip = lax.ppermute(to_chip, ROW, next_chip)
    from_core = lax.ppermute(to_core, "row_2", SWAP)

    scaled, query, key, value = call(
        load_kernel, [block] * 4, [VMEM] * 3 + [HBM] * 4, [pltpu.SemaphoreType.DMA((4,)), pltpu.VMEM((tokens, width), BF)]
    )(count, to_core, rates, aim, query, key, value)
    attend = lambda *refs: attend_kernel(rows, cols, n_row * rows, *refs)
    own = call(attend, ((2, tokens, width), BF), [VMEM] * 8)(count, reach, query, key, value, from_core, from_chip, scaled)
    other = lax.ppermute(own, "row_2", SWAP)
    ws = w_first[0], w_third[0], w_second[0]
    ahead = lambda *refs: forward_kernel(n_plane, n_near, *refs)
    back, gated, old = call(ahead, [((2, tokens, width), BF), ((tokens, width // 2), BF), ((few, 3 * width), F32)], [VMEM] * 4)(own, *ws)
    planes, nears = led(PLANE, n_plane - 1), led("near", n_near - 2)
    planes_late, nears_late = led(PLANE, n_plane - 2), led("near", n_near - 1)
    grads = lambda *refs: grads_kernel(planes, *refs)
    part = call(grads, ((n_plane, 3 * share, width), BF), [VMEM] * 7)(own, back, gated, other, *ws)
    part = exchange(part, PLANE, planes)
    spread = lambda *refs: spread_kernel(nears, few, *refs)
    part = call(spread, ((n_near, few, 3 * width + 128), BF), [VMEM] * 2)(count, part)
    part = exchange(part, "near", nears)
    part = call(gather_kernel, ((n_far, few, 3 * width + 128), BF), [VMEM])(part)
    part = exchange(part, "far", led("far", n_far // 2))
    new = call(renew_kernel, ((n_near, few, 3 * width), BF), [VMEM] * 2)(part, old)
    new = exchange(new, "near", nears_late)
    lines = call(lambda *refs: order_kernel(nears_late, *refs), ((n_plane, 3 * share, width), BF), [VMEM])(new)
    mine = exchange(lines, PLANE, planes_late)
    theirs = lax.ppermute(mine, "row_2", SWAP)
    part = call(lambda *refs: half_kernel(planes_late, *refs), ((2, tokens, width), F32), [VMEM] * 2)(own, mine)
    scratch = [pltpu.VMEM((tokens, width), BF), pltpu.SemaphoreType.DMA((2,))]
    out = call(lambda *refs: apply_kernel(planes_late, *refs), block, [VMEM] * 4, scratch, HBM)(own, part, mine, theirs)
    return out.reshape(1, rows, cols, width)


def solution(mesh):
    torus = Mesh(
        mesh.devices.reshape(mesh.shape["head"], mesh.shape["view"] // 4, 4, 2, 4, 2),
        ("head", "far", "near", "row_0", "row_1", "row_2"),
    )
    views = ("far", "near")
    feats = P(views, ROW, None, "head")
    heads = P("head", None, None)
    return jax.shard_map(
        per_device,
        mesh=torus,
        in_specs=(feats, feats, feats, feats, P(views, "head", ROW), P(ROW), P(views), heads, heads, heads),
        out_specs=feats,
        check_vma=False,
    )
```
